512 devices in a mesh: cuts: 16 (over x_lo, z), space: 32 (over y, x_hi, core).
Axes of the slice: x: 4 (x_hi: 2, x_lo: 2; x = x_hi * 2 + x_lo), y: 8, z: 8, core: 2. Of those that a mesh axis runs over, the one named last changes fastest.
Arguments:
- old_starts: float32 [16, 5, 64, 16, 256], P('cuts', None, 'space'), may hold values from -6 to 6
- initial: float32 [5, 64, 16, 256], P(None, 'space'), may hold values from -6 to 6
- blade_force: float32 [5, 64, 16, 256], P(None, 'space'), may hold values from -6 to 6
- blade_owner: int32 [16, 3], replicated, may hold values from 0 to 31, as said below
Outputs:
- new_ends: float32 [16, 5, 64, 16, 256], P('cuts', None, 'space')
- jumps: float32 [16, 5, 64, 16, 256], P('cuts', None, 'space')
The draws below stay inside these ranges and needn't reach their ends.
Inputs may be any that keep to these rules, and one draw needn't show every extreme that they name: `blade_owner`: both the smallest and the largest block index occur in every draw.
All inputs are finite; a program needn't handle non-finite values.
Results may differ from the reference program's by a relative error of at most 0.0001.
Values sent between devices are 32-bit elements; how exact they have to be, the bound alone decides.
A program may use at most 64 MiB of HBM per device.

```python
import jax
import jax.numpy as jnp

NVAR = 5
CX = 2
NY = 16
NZ = 256
STEPS = 3
SLICES = 16
NX = 64
N_SPACE = 32


def draw_blade_owner(key, part):
    total = SLICES * STEPS
    first_key = jax.random.fold_in(key, 11)
    second_key = jax.random.fold_in(key, 12)
    third_key = jax.random.fold_in(key, 13)
    values = jax.random.randint(first_key, (total,), 0, N_SPACE)
    spot = jax.random.randint(second_key, (), 0, total)
    other = (spot + 1 + jax.random.randint(third_key, (), 0, total - 1)) % total
    values = values.at[spot].set(N_SPACE - 1)
    values = values.at[other].set(0)
    return values.reshape(SLICES, STEPS).astype(jnp.int32)


def steps_of(own_key, dims, pieces, low, top_value):
    gain, own = 1.0, jax.random.fold_in(own_key, 6)
    for position, shards_of in pieces:
        heights = jnp.exp(jax.random.uniform(jax.random.fold_in(own, position), (shards_of,), jnp.float32, low / len(pieces), top_value / len(pieces)))
        gain = gain * jnp.repeat(heights, dims[position] // shards_of).reshape([-1 if axis == position else 1 for axis in range(len(dims))])
    return gain


def centred(stream_key, extent, deviation, reach, pieces=(), kind=jnp.bfloat16):
    drawn = deviation * jax.random.normal(stream_key, extent, jnp.float32)
    if pieces:
        drawn = drawn * steps_of(stream_key, extent, pieces, -0.22, 0.18)
    return jnp.clip(drawn, -reach, reach).astype(kind)


def setup_inputs(seed: int = 0) -> dict:
    streams_of = jax.random.split(jax.random.key(seed), 5)
    return {
        "old_starts": centred(streams_of[0], (SLICES, NVAR, NX, NY, NZ), 1.0, 6.0, ((0, 16), (2, 32)), jnp.float32),
        "initial": centred(streams_of[1], (NVAR, NX, NY, NZ), 1.0, 6.0, ((1, 32),), jnp.float32),
        "blade_force": centred(streams_of[2], (NVAR, NX, NY, NZ), 1.0, 6.0, ((1, 32),), jnp.float32),
        "blade_owner": draw_blade_owner(jax.random.fold_in(streams_of[4], 71), 0),
    }


mach = 0.3
courant = 0.2
coarse_courant = 0.3


def flux_rate(padded, ratio):
    center = padded[:, 1:-1]
    x_diff = padded[:, 2:] - padded[:, :-2]
    x_second = padded[:, 2:] - 2.0 * center + padded[:, :-2]
    y_upper = jnp.roll(center, -1, axis=2)
    y_lower = jnp.roll(center, 1, axis=2)
    z_upper = jnp.roll(center, -1, axis=3)
    z_lower = jnp.roll(center, 1, axis=3)
    y_diff = y_upper - y_lower
    z_diff = z_upper - z_lower
    y_second = y_upper - 2.0 * center + y_lower
    z_second = z_upper - 2.0 * center + z_lower
    divergence = x_diff[1] + y_diff[2] + z_diff[3]
    coupling = jnp.stack([divergence, x_diff[4], y_diff[4], z_diff[4], divergence])
    return -0.5 * ratio * (mach * x_diff + coupling) + 0.5 * ratio * ((mach + 1.0) * x_second + y_second + z_second)


def pad_first(state):
    return jnp.pad(state, ((0, 0), (1, 1), (0, 0), (0, 0)))


def restrict(field):
    shape = field.shape
    blocks = field.reshape(shape[0], shape[1] // 2, 2, shape[2] // 2, 2, shape[3] // 2, 2)
    return jnp.mean(blocks, axis=(2, 4, 6))


def prolong(field):
    return jnp.repeat(jnp.repeat(jnp.repeat(field, 2, axis=1), 2, axis=2), 2, axis=3)


def coarse_step(coarse, source):
    return coarse + flux_rate(pad_first(coarse), coarse_courant) + source


def reference(old_starts, initial, blade_force, blade_owner):
    block_of = jnp.arange(NX) // CX
    coarse_block = jnp.arange(NX // 2) // (CX // 2)
    restricted_force = restrict(blade_force)
    ends = []
    jumps = []
    previous_fine = initial
    start = initial
    for index in range(SLICES):
        old = old_starts[index]
        state = old
        counts = jnp.zeros((NX // 2,), jnp.float32)
        for step in range(STEPS):
            owner = blade_owner[index, step]
            mask = (block_of == owner).astype(jnp.float32)[None, :, None, None]
            counts = counts + (coarse_block == owner).astype(jnp.float32)
            source = courant * mask * blade_force
            first = state + flux_rate(pad_first(state), courant) + source
            state = 0.5 * (state + first + flux_rate(pad_first(first), courant) + source)
        coarse_source = courant * counts[None, :, None, None] * restricted_force
        g_old = prolong(coarse_step(restrict(old), coarse_source))
        correction = state - g_old
        end = prolong(coarse_step(restrict(start), coarse_source)) + correction
        jumps.append(old - previous_fine)
        previous_fine = state
        ends.append(end)
        start = end
    return jnp.stack(ends), jnp.stack(jumps)
```

```python
import functools

import jax
import jax.numpy as jnp
import numpy as np
from jax import lax
from jax.experimental import pallas as pl
from jax.experimental.pallas import tpu as pltpu
from jax.sharding import PartitionSpec as P

MESH = pl.DeviceIdType.MESH
HIGHEST = lax.Precision.HIGHEST

STEPS = 3
NVAR = 5
NY = 16
NZ = 256
SPACE = 32
CUTS = 16
LANES = 128
ROWS = 2 * NVAR * NY

mach = 0.3
courant = 0.2
coarse_courant = 0.3


def wave(count, k, phase):
    angle = 2.0 * np.pi * k * np.arange(count) / count
    v = np.cos(angle) if phase == 0 else np.sin(angle)
    return v / np.sqrt(np.sum(v * v))


def group_waves(g):
    if g == 0:
        fine = [(0, 0), (64, 0), (128, 0), (64, 1)]
        coarse = [(0, 0), (64, 0)]
    else:
        fine = [(g, 0), (128 - g, 0), (g, 1), (128 - g, 1)]
        coarse = [(g, 0), (g, 1)]
    return fine, coarse


def make_tables():
    half = NZ // 2
    restrict_z = np.zeros((half, NZ))
    for j in range(half):
        restrict_z[j, 2 * j : 2 * j + 2] = 0.5
    forward = np.zeros((8, SPACE, NZ))
    back_coarse = np.zeros((4, SPACE, NZ))
    lanes = np.zeros((SPACE, 16, 8, NY))
    even = (np.arange(NY) % 2 == 0).astype(np.float64)
    for t in range(SPACE):
        for q in range(2):
            fine, coarse = group_waves(t + 32 * q)
            basis = [wave(NZ, *w) for w in fine]
            coarse_basis = [wave(half, *w) for w in coarse]
            for i in range(4):
                slot = q + 2 * i
                forward[slot, t] = basis[i]
                upper, lower = np.roll(basis[i], -1), np.roll(basis[i], 1)
                lanes[t, 0, slot] = basis[i] @ (upper + lower) - 2.0
                partner = basis[(i + 2) % 4]
                lanes[t, 1, slot] = basis[i] @ (np.roll(partner, -1) - np.roll(partner, 1))
            for i in range(2):
                slot = q + 4 * i
                back_coarse[q + 2 * i, t] = np.repeat(coarse_basis[i], 2)
                upper, lower = np.roll(coarse_basis[i], -1), np.roll(coarse_basis[i], 1)
                lanes[t, 2, slot] = coarse_basis[i] @ (upper + lower) - 2.0
                partner = coarse_basis[1 - i]
                lanes[t, 3, slot] = coarse_basis[i] @ (np.roll(partner, -1) - np.roll(partner, 1))
                for j in range(4):
                    source = (2 * i + j) % 4
                    lanes[t, 4 + j, slot] = 0.25 * (coarse_basis[i] @ (restrict_z @ basis[source])) * even
                lanes[t, 8, slot] = even
    return (
        forward.reshape(8 * SPACE, NZ).astype(np.float32),
        back_coarse.reshape(4 * SPACE, NZ).astype(np.float32),
        lanes.reshape(SPACE, 16, LANES).astype(np.float32),
    )


FORWARD, BACK_COARSE, LANE_TABLE = make_tables()


def turn(a, shift):
    return pltpu.roll(a, shift % LANES, 1)


def swap_blocks(arrays):
    arrays = list(arrays)
    block = lax.broadcasted_iota(jnp.int32, arrays[0].shape, 1) // NY
    for bit in (4, 2, 1):
        low = (block // bit) % 2 == 0
        for i in range(8):
            if i & bit == 0:
                a, b = arrays[i], arrays[i + bit]
                arrays[i] = jnp.where(low, a, turn(b, NY * bit))
                arrays[i + bit] = jnp.where(low, turn(a, -NY * bit), b)
    return arrays


def along_y(a, step):
    y = lax.broadcasted_iota(jnp.int32, a.shape, 1) % NY
    upper = jnp.where(y >= NY - step, turn(a, NY - step), turn(a, -step))
    lower = jnp.where(y < step, turn(a, step - NY), turn(a, step))
    return upper, lower


def below(a):
    row = lax.broadcasted_iota(jnp.int32, a.shape, 0)
    return jnp.where(row == 0, 0.0, pltpu.roll(a, 1, 0))


def above(a):
    row = lax.broadcasted_iota(jnp.int32, a.shape, 0)
    return jnp.where(row == a.shape[0] - 1, 0.0, pltpu.roll(a, a.shape[0] - 1, 0))


def rate_of(center, x_upper, x_lower, step, second_z, first_z, ratio):
    half = 0.5 * ratio
    own = second_z - 2.0 * (mach + 1.0) - 2.0
    rates = []
    ys = [along_y(center[v], step) for v in range(NVAR)]
    for v in range(NVAR):
        rates.append(x_upper[v] + (2.0 * mach + 1.0) * x_lower[v] + ys[v][0] + ys[v][1] + own * center[v])
    divergence = (x_upper[1] - x_lower[1]) + (ys[2][0] - ys[2][1]) + first_z * turn(center[3], 64)
    rates[0] = rates[0] - divergence
    rates[1] = rates[1] - (x_upper[4] - x_lower[4])
    rates[2] = rates[2] - (ys[4][0] - ys[4][1])
    rates[3] = rates[3] - first_z * turn(center[4], 64)
    rates[4] = rates[4] - divergence
    return [half * r for r in rates]


def kernel(
    old_ref, init_ref, force_ref, owner_ref, forward_ref, back_ref, table_ref,
    ends_ref, jumps_ref,
    stacked, out1, in1, state, first, out2, in2, out3, in3, packed, gathered, fine, before,
    send1, recv1, send2, recv2, send3, recv3, send4, recv4, send5, recv5,
):
    n = lax.axis_index("cuts")
    s = lax.axis_index("space")

    barrier = pltpu.get_barrier_semaphore()

    def greet_space(k, c):
        pl.semaphore_signal(barrier, inc=1, device_id={"space": lax.rem(s + k, SPACE)}, device_id_type=MESH)
        return c

    def greet_cuts(k, c):
        pl.semaphore_signal(barrier, inc=1, device_id={"cuts": lax.rem(n + k, CUTS)}, device_id_type=MESH)
        return c

    lax.fori_loop(1, SPACE, greet_space, 0)
    lax.fori_loop(1, CUTS, greet_cuts, 0)

    stacked[0:ROWS] = old_ref[...]
    stacked[ROWS : 2 * ROWS] = force_ref[...]
    row = lax.broadcasted_iota(jnp.int32, (NY, NZ), 0)
    sums = []
    for v in range(NVAR):
        both = init_ref[2 * v * NY : (2 * v + 1) * NY] + init_ref[(2 * v + 1) * NY : (2 * v + 2) * NY]
        sums.append(both + pltpu.roll(both, NY - 1, 0))
    sums.append(jnp.zeros((NY, NZ), jnp.float32))
    for pair in range(3):
        merged = jnp.where(row % 2 == 0, sums[2 * pair], pltpu.roll(sums[2 * pair + 1], 1, 0))
        stacked[2 * ROWS + pair * NY : 2 * ROWS + (pair + 1) * NY] = merged
    stacked[2 * ROWS + 3 * NY :] = jnp.zeros((NY, NZ), jnp.float32)
    for tile in range(3):
        modes = lax.dot_general(
            forward_ref[...],
            stacked[tile * LANES : (tile + 1) * LANES],
            (((1,), (1,)), ((), ())),
            precision=HIGHEST,
            preferred_element_type=jnp.float32,
        )
        by_row = swap_blocks([modes[m * SPACE : (m + 1) * SPACE] for m in range(8)])
        for r in range(8):
            for j in range(4):
                out1[pl.ds(24 * 8 * j + 8 * tile + r, 8, stride=24), :] = by_row[r][8 * j : 8 * j + 8]

    pl.semaphore_wait(barrier, SPACE + CUTS - 2)

    def exchange(source, target, rows, send, recv):
        def piece(ref, i):
            return ref.at[pl.ds(pl.multiple_of(i * rows, 8), rows), :]

        def start(k, c):
            peer = lax.rem(s + k, SPACE)
            pltpu.make_async_remote_copy(
                piece(source, peer), piece(target, s), send.at[peer], recv.at[s],
                device_id={"space": peer}, device_id_type=MESH,
            ).start()
            return c

        def settle(k, c):
            peer = lax.rem(s + k, SPACE)
            pltpu.make_async_remote_copy(
                piece(source, peer), piece(target, peer), send.at[peer], recv.at[peer],
                device_id={"space": peer}, device_id_type=MESH,
            ).wait()
            return c

        def begin():
            lax.fori_loop(1, SPACE, start, 0)
            mine = pl.ds(pl.multiple_of(s * rows, 8), rows)
            target[mine, :] = source[mine, :]

        def finish():
            lax.fori_loop(1, SPACE, settle, 0)

        return begin, finish

    begin1, finish1 = exchange(out1, in1, 24, send1, recv1)
    begin1()
    finish1()

    table = table_ref[s]
    lane = [jnp.broadcast_to(table[i : i + 1], (SPACE, LANES)) for i in range(9)]

    def arrived(r):
        return jnp.concatenate([in1[pl.ds(24 * 8 * j + r, 8, stride=24), :] for j in range(4)], axis=0)

    def restrict_modes(t):
        return lane[4] * t + lane[5] * turn(t, 96) + lane[6] * turn(t, 64) + lane[7] * turn(t, 32)

    def restrict(q0, q1):
        t = q0 + q1
        return restrict_modes(t + turn(t, -1))

    def fine_rate(ref):
        q = [[ref[(2 * v + i) * SPACE : (2 * v + i + 1) * SPACE] for i in range(2)] for v in range(NVAR)]
        low = rate_of(
            [q[v][0] for v in range(NVAR)], [q[v][1] for v in range(NVAR)], [below(q[v][1]) for v in range(NVAR)],
            1, lane[0], lane[1], courant,
        )
        high = rate_of(
            [q[v][1] for v in range(NVAR)], [above(q[v][0]) for v in range(NVAR)], [q[v][0] for v in range(NVAR)],
            1, lane[0], lane[1], courant,
        )
        return q, [[low[v], high[v]] for v in range(NVAR)]

    def coarse_advance(c):
        r = rate_of(c, [above(a) for a in c], [below(a) for a in c], 2, lane[2], lane[3], coarse_courant)
        return [c[v] + r[v] for v in range(NVAR)]

    for r in range(2 * NVAR):
        state[r * SPACE : (r + 1) * SPACE] = arrived(r)
    place = lax.broadcasted_iota(jnp.int32, (SPACE, LANES), 0)
    hits = [(place == owner_ref[n, k]).astype(jnp.float32) for k in range(STEPS)]
    old_coarse = [restrict(arrived(2 * v), arrived(2 * v + 1)) for v in range(NVAR)]
    for k in range(STEPS):
        q, rates = fine_rate(state)
        scale = courant * hits[k]
        for v in range(NVAR):
            for i in range(2):
                at = slice((2 * v + i) * SPACE, (2 * v + i + 1) * SPACE)
                source = scale * arrived(2 * NVAR + 2 * v + i)
                first[at] = q[v][i] + rates[v][i] + source
        q1, rates1 = fine_rate(first)
        for v in range(NVAR):
            for i in range(2):
                at = slice((2 * v + i) * SPACE, (2 * v + i + 1) * SPACE)
                source = scale * arrived(2 * NVAR + 2 * v + i)
                state[at] = 0.5 * (state[at] + q1[v][i] + rates1[v][i] + source)

    final = [[state[(2 * v + i) * SPACE : (2 * v + i + 1) * SPACE] for i in range(2)] for v in range(NVAR)]
    count = hits[0] + hits[1] + hits[2]
    coarse_source = [
        courant * count * restrict(arrived(2 * NVAR + 2 * v), arrived(2 * NVAR + 2 * v + 1)) for v in range(NVAR)
    ]
    guess_old = [a + b for a, b in zip(coarse_advance(old_coarse), coarse_source)]
    for v in range(NVAR):
        gain = coarse_source[v] + restrict(final[v][0], final[v][1]) - guess_old[v]
        packed[8 * v : 8 * v + 8] = (
            gain[0:8] + turn(gain[8:16], 1) + turn(gain[16:24], 32) + turn(gain[24:32], 33)
        )

    def send_gain(k, c):
        pltpu.make_async_remote_copy(
            packed, gathered.at[n], send4.at[k], recv4.at[n], device_id={"cuts": n + k}, device_id_type=MESH
        ).start()
        return c

    def sent_gain(k, c):
        pltpu.make_async_remote_copy(
            packed, gathered.at[n], send4.at[k], recv4.at[n], device_id={"cuts": n + k}, device_id_type=MESH
        ).wait_send()
        return c

    lax.fori_loop(1, CUTS - n, send_gain, 0)

    for v in range(NVAR):
        for i in range(2):
            for j in range(4):
                out2[pl.ds(16 * 8 * j + 2 * v + i, 8, stride=16), :] = final[v][i][8 * j : 8 * j + 8]
    begin2, finish2 = exchange(out2, in2, 16, send2, recv2)
    begin2()

    useful = lane[8][0:8]

    def advance(m, c):
        pltpu.make_async_remote_copy(
            packed, gathered.at[m], send4.at[0], recv4.at[m], device_id={"cuts": m}, device_id_type=MESH
        ).wait_recv()
        moved = coarse_advance(list(c))
        result = []
        for v in range(NVAR):
            g = gathered[m, 8 * v : 8 * v + 8]
            parts = [useful * g, useful * turn(g, -1), useful * turn(g, -32), useful * turn(g, -33)]
            result.append(moved[v] + jnp.concatenate(parts, axis=0))
        return tuple(result)

    begin_coarse = []
    for v in range(NVAR):
        a = arrived(4 * NVAR + v // 2)
        begin_coarse.append(restrict_modes(turn(a, -1) if v % 2 else a))
    start = lax.fori_loop(0, n, advance, tuple(begin_coarse))
    guess_new = [a + b for a, b in zip(coarse_advance(list(start)), coarse_source)]
    for v in range(NVAR):
        change = guess_new[v] - guess_old[v]
        change = change + turn(change, 1)
        for j in range(4):
            out3[pl.ds(8 * 8 * j + v, 8, stride=8), :] = change[8 * j : 8 * j + 8]
    begin3, finish3 = exchange(out3, in3, 8, send3, recv3)
    begin3()

    finish2()
    halves = []
    for tile in range(2):
        rows = []
        for r in range(8):
            from_row = min(8 * tile + r, 2 * NVAR - 1)
            rows.append(
                jnp.concatenate([in2[pl.ds(16 * 8 * j + from_row, 8, stride=16), :] for j in range(4)], axis=0)
            )
        halves.append(jnp.concatenate(swap_blocks(rows), axis=0).T)
    modes = jnp.concatenate([halves[0], halves[1][: ROWS - LANES]], axis=0)
    fine[...] = jnp.dot(modes, forward_ref[...], precision=HIGHEST, preferred_element_type=jnp.float32)

    def to_next():
        return pltpu.make_async_remote_copy(
            fine, before, send5, recv5, device_id={"cuts": lax.rem(n + 1, CUTS)}, device_id_type=MESH
        )

    @pl.when(n < CUTS - 1)
    def _():
        to_next().start()

    finish3()
    rows = []
    for v in range(8):
        from_row = min(v, NVAR - 1)
        rows.append(jnp.concatenate([in3[pl.ds(8 * 8 * j + from_row, 8, stride=8), :] for j in range(4)], axis=0))
    by_mode = swap_blocks(rows)
    change = jnp.concatenate([by_mode[0], by_mode[1], by_mode[4], by_mode[5]], axis=0).T
    change = jnp.dot(change[: NVAR * NY], back_ref[...], precision=HIGHEST, preferred_element_type=jnp.float32)
    for v in range(NVAR):
        for i in range(2):
            at = slice((2 * v + i) * NY, (2 * v + i + 1) * NY)
            ends_ref[at] = fine[at] + change[v * NY : (v + 1) * NY]

    lax.fori_loop(1, CUTS - n, sent_gain, 0)

    @pl.when(n == 0)
    def _():
        jumps_ref[...] = old_ref[...] - init_ref[...]

    @pl.when(n > 0)
    def _():
        to_next().wait_recv()
        jumps_ref[...] = old_ref[...] - before[...]

    @pl.when(n < CUTS - 1)
    def _():
        to_next().wait_send()


def body(old_starts, initial, blade_force, blade_owner):
    vmem = pl.BlockSpec(memory_space=pltpu.VMEM)
    smem = pl.BlockSpec(memory_space=pltpu.SMEM)
    f32 = jnp.float32
    dma = pltpu.SemaphoreType.DMA
    ends, jumps = pl.pallas_call(
        kernel,
        out_shape=[jax.ShapeDtypeStruct((ROWS, NZ), f32)] * 2,
        in_specs=[vmem, vmem, vmem, smem, vmem, vmem, vmem],
        out_specs=[vmem, vmem],
        scratch_shapes=[
            pltpu.VMEM((3 * LANES, NZ), f32),
            pltpu.VMEM((SPACE * 24, LANES), f32),
            pltpu.VMEM((SPACE * 24, LANES), f32),
            pltpu.VMEM((2 * NVAR * SPACE, LANES), f32),
            pltpu.VMEM((2 * NVAR * SPACE, LANES), f32),
            pltpu.VMEM((SPACE * 16, LANES), f32),
            pltpu.VMEM((SPACE * 16, LANES), f32),
            pltpu.VMEM((SPACE * 8, LANES), f32),
            pltpu.VMEM((SPACE * 8, LANES), f32),
            pltpu.VMEM((8 * NVAR, LANES), f32),
            pltpu.VMEM((CUTS, 8 * NVAR, LANES), f32),
            pltpu.VMEM((ROWS, NZ), f32),
            pltpu.VMEM((ROWS, NZ), f32),
            dma((SPACE,)),
            dma((SPACE,)),
            dma((SPACE,)),
            dma((SPACE,)),
            dma((SPACE,)),
            dma((SPACE,)),
            dma((CUTS,)),
            dma((CUTS,)),
            dma,
            dma,
        ],
        compiler_params=pltpu.CompilerParams(
            collective_id=0, has_side_effects=True, vmem_limit_bytes=24 * 2**20
        ),
    )(
        old_starts.reshape(ROWS, NZ),
        initial.reshape(ROWS, NZ),
        blade_force.reshape(ROWS, NZ),
        blade_owner,
        jnp.asarray(FORWARD),
        jnp.asarray(BACK_COARSE),
        jnp.asarray(LANE_TABLE),
    )
    shape = old_starts.shape
    return ends.reshape(shape), jumps.reshape(shape)


def solution(mesh):
    placed = (
        P("cuts", None, "space", None, None),
        P(None, "space", None, None),
        P(None, "space", None, None),
        P(),
    )
    return jax.shard_map(
        body,
        mesh=mesh,
        in_specs=placed,
        out_specs=(P("cuts", None, "space", None, None), P("cuts", None, "space", None, None)),
        check_vma=False,
    )
```

```python
import functools

import jax
import jax.numpy as jnp
import numpy as np
from jax import lax
from jax.experimental import pallas as pl
from jax.experimental.pallas import tpu as pltpu
from jax.sharding import PartitionSpec as P

MESH = pl.DeviceIdType.MESH
HIGHEST = lax.Precision.HIGHEST

STEPS = 3
NVAR = 5
NY = 16
NZ = 256
SPACE = 32
CUTS = 16
LANES = 128
ROWS = 2 * NVAR * NY

mach = 0.3
courant = 0.2
coarse_courant = 0.3


def wave(count, k, phase):
    angle = 2.0 * np.pi * k * np.arange(count) / count
    v = np.cos(angle) if phase == 0 else np.sin(angle)
    return v / np.sqrt(np.sum(v * v))


def group_waves(g):
    if g == 0:
        fine = [(0, 0), (64, 0), (128, 0), (64, 1)]
        coarse = [(0, 0), (64, 0)]
    else:
        fine = [(g, 0), (128 - g, 0), (g, 1), (128 - g, 1)]
        coarse = [(g, 0), (g, 1)]
    return fine, coarse


def make_tables():
    half = NZ // 2
    restrict_z = np.zeros((half, NZ))
    for j in range(half):
        restrict_z[j, 2 * j : 2 * j + 2] = 0.5
    forward = np.zeros((8, SPACE, NZ))
    back_coarse = np.zeros((4, SPACE, NZ))
    lanes = np.zeros((SPACE, 16, 8, NY))
    even = (np.arange(NY) % 2 == 0).astype(np.float64)
    for t in range(SPACE):
        for q in range(2):
            fine, coarse = group_waves(t + 32 * q)
            basis = [wave(NZ, *w) for w in fine]
            coarse_basis = [wave(half, *w) for w in coarse]
            for i in range(4):
                slot = q + 2 * i
                forward[slot, t] = basis[i]
                upper, lower = np.roll(basis[i], -1), np.roll(basis[i], 1)
                lanes[t, 0, slot] = basis[i] @ (upper + lower) - 2.0
                partner = basis[(i + 2) % 4]
                lanes[t, 1, slot] = basis[i] @ (np.roll(partner, -1) - np.roll(partner, 1))
            for i in range(2):
                slot = q + 4 * i
                back_coarse[q + 2 * i, t] = np.repeat(coarse_basis[i], 2)
                upper, lower = np.roll(coarse_basis[i], -1), np.roll(coarse_basis[i], 1)
                lanes[t, 2, slot] = coarse_basis[i] @ (upper + lower) - 2.0
                partner = coarse_basis[1 - i]
                lanes[t, 3, slot] = coarse_basis[i] @ (np.roll(partner, -1) - np.roll(partner, 1))
                for j in range(4):
                    source = (2 * i + j) % 4
                    lanes[t, 4 + j, slot] = 0.25 * (coarse_basis[i] @ (restrict_z @ basis[source])) * even
                lanes[t, 8, slot] = even
    return (
        forward.reshape(8 * SPACE, NZ).astype(np.float32),
        back_coarse.reshape(4 * SPACE, NZ).astype(np.float32),
        lanes.reshape(SPACE, 16, LANES).astype(np.float32),
    )


FORWARD, BACK_COARSE, LANE_TABLE = make_tables()


def turn(a, shift):
    return pltpu.roll(a, shift % LANES, 1)


def swap_blocks(arrays):
    arrays = list(arrays)
    block = lax.broadcasted_iota(jnp.int32, arrays[0].shape, 1) // NY
    for bit in (4, 2, 1):
        low = (block // bit) % 2 == 0
        for i in range(8):
            if i & bit == 0:
                a, b = arrays[i], arrays[i + bit]
                arrays[i] = jnp.where(low, a, turn(b, NY * bit))
                arrays[i + bit] = jnp.where(low, turn(a, -NY * bit), b)
    return arrays


def along_y(a, step):
    y = lax.broadcasted_iota(jnp.int32, a.shape, 1) % NY
    upper = jnp.where(y >= NY - step, turn(a, NY - step), turn(a, -step))
    lower = jnp.where(y < step, turn(a, step - NY), turn(a, step))
    return upper, lower


def below(a):
    row = lax.broadcasted_iota(jnp.int32, a.shape, 0)
    return jnp.where(row == 0, 0.0, pltpu.roll(a, 1, 0))


def above(a):
    row = lax.broadcasted_iota(jnp.int32, a.shape, 0)
    return jnp.where(row == a.shape[0] - 1, 0.0, pltpu.roll(a, a.shape[0] - 1, 0))


def rate_of(center, x_upper, x_lower, step, second_z, first_z, ratio):
    half = 0.5 * ratio
    own = second_z - 2.0 * (mach + 1.0) - 2.0
    rates = []
    ys = [along_y(center[v], step) for v in range(NVAR)]
    for v in range(NVAR):
        rates.append(x_upper[v] + (2.0 * mach + 1.0) * x_lower[v] + ys[v][0] + ys[v][1] + own * center[v])
    divergence = (x_upper[1] - x_lower[1]) + (ys[2][0] - ys[2][1]) + first_z * turn(center[3], 64)
    rates[0] = rates[0] - divergence
    rates[1] = rates[1] - (x_upper[4] - x_lower[4])
    rates[2] = rates[2] - (ys[4][0] - ys[4][1])
    rates[3] = rates[3] - first_z * turn(center[4], 64)
    rates[4] = rates[4] - divergence
    return [half * r for r in rates]


def kernel(
    old_hbm, init_hbm, force_hbm, owner_hbm, forward_hbm, back_hbm, table_hbm,
    fine_hbm, change_hbm, before_hbm,
    init_ref, owner_ref, forward_ref, back_ref, table, stacked, out1, in1, state, first, out2, in2, out3, in3, packed, gathered, fine, change_ref,
    load, send1, recv1, send2, recv2, send3, recv3, send4, recv4, send5, recv5, store,
):
    n = lax.axis_index("cuts")
    s = lax.axis_index("space")

    def peer_of(k):
        return lax.rem(s + SPACE // 2 + (k // 2) * (1 - 2 * lax.rem(k, 2)), SPACE)

    old_ref = stacked.at[0:ROWS]
    loads = [
        pltpu.make_async_copy(source, target, load.at[i])
        for i, (source, target) in enumerate(
            (
                (forward_hbm, forward_ref),
                (old_hbm, old_ref),
                (force_hbm, stacked.at[ROWS : 2 * ROWS]),
                (init_hbm, init_ref),
                (owner_hbm, owner_ref),
                (table_hbm.at[s], table),
                (back_hbm, back_ref),
            )
        )
    ]
    for copy in loads:
        copy.start()

    barrier = pltpu.get_barrier_semaphore()

    def greet_space(k, c):
        pl.semaphore_signal(barrier, inc=1, device_id={"space": peer_of(k)}, device_id_type=MESH)
        return c

    def greet_cuts(k, c):
        pl.semaphore_signal(barrier, inc=1, device_id={"cuts": lax.rem(n + k, CUTS)}, device_id_type=MESH)
        return c

    lax.fori_loop(1, SPACE, greet_space, 0)
    lax.fori_loop(1, CUTS, greet_cuts, 0)

    for copy in loads[:4]:
        copy.wait()
    row = lax.broadcasted_iota(jnp.int32, (NY, NZ), 0)
    sums = []
    for v in range(NVAR):
        both = init_ref[2 * v * NY : (2 * v + 1) * NY] + init_ref[(2 * v + 1) * NY : (2 * v + 2) * NY]
        sums.append(both + pltpu.roll(both, NY - 1, 0))
    sums.append(jnp.zeros((NY, NZ), jnp.float32))
    for pair in range(3):
        merged = jnp.where(row % 2 == 0, sums[2 * pair], pltpu.roll(sums[2 * pair + 1], 1, 0))
        stacked[2 * ROWS + pair * NY : 2 * ROWS + (pair + 1) * NY] = merged
    stacked[2 * ROWS + 3 * NY :] = jnp.zeros((NY, NZ), jnp.float32)
    for tile in range(3):
        modes = lax.dot_general(
            forward_ref[...],
            stacked[tile * LANES : (tile + 1) * LANES],
            (((1,), (1,)), ((), ())),
            precision=HIGHEST,
            preferred_element_type=jnp.float32,
        )
        by_row = swap_blocks([modes[m * SPACE : (m + 1) * SPACE] for m in range(8)])
        for r in range(8):
            for j in range(4):
                out1[pl.ds(24 * 8 * j + 8 * tile + r, 8, stride=24), :] = by_row[r][8 * j : 8 * j + 8]

    pl.semaphore_wait(barrier, SPACE + CUTS - 2)

    def exchange(source, target, rows, send, recv):
        def piece(ref, i):
            return ref.at[pl.ds(pl.multiple_of(i * rows, 8), rows), :]

        def start(k, c):
            peer = peer_of(k)
            pltpu.make_async_remote_copy(
                piece(source, peer), piece(target, s), send.at[peer], recv.at[s],
                device_id={"space": peer}, device_id_type=MESH,
            ).start()
            return c

        def settle(k, c):
            peer = peer_of(k)
            pltpu.make_async_remote_copy(
                piece(source, peer), piece(target, peer), send.at[peer], recv.at[peer],
                device_id={"space": peer}, device_id_type=MESH,
            ).wait()
            return c

        def begin():
            lax.fori_loop(1, SPACE, start, 0)
            mine = pl.ds(pl.multiple_of(s * rows, 8), rows)
            target[mine, :] = source[mine, :]

        def finish():
            lax.fori_loop(1, SPACE, settle, 0)

        return begin, finish

    begin1, finish1 = exchange(out1, in1, 24, send1, recv1)
    begin1()
    for copy in loads[4:]:
        copy.wait()
    finish1()

    lane = [jnp.broadcast_to(table[i : i + 1], (SPACE, LANES)) for i in range(9)]

    def arrived(r):
        return jnp.concatenate([in1[pl.ds(24 * 8 * j + r, 8, stride=24), :] for j in range(4)], axis=0)

    def restrict_modes(t):
        return lane[4] * t + lane[5] * turn(t, 96) + lane[6] * turn(t, 64) + lane[7] * turn(t, 32)

    def restrict(q0, q1):
        t = q0 + q1
        return restrict_modes(t + turn(t, -1))

    def fine_rate(ref):
        q = [[ref[(2 * v + i) * SPACE : (2 * v + i + 1) * SPACE] for i in range(2)] for v in range(NVAR)]
        low = rate_of(
            [q[v][0] for v in range(NVAR)], [q[v][1] for v in range(NVAR)], [below(q[v][1]) for v in range(NVAR)],
            1, lane[0], lane[1], courant,
        )
        high = rate_of(
            [q[v][1] for v in range(NVAR)], [above(q[v][0]) for v in range(NVAR)], [q[v][0] for v in range(NVAR)],
            1, lane[0], lane[1], courant,
        )
        return q, [[low[v], high[v]] for v in range(NVAR)]

    def coarse_advance(c):
        r = rate_of(c, [above(a) for a in c], [below(a) for a in c], 2, lane[2], lane[3], coarse_courant)
        return [c[v] + r[v] for v in range(NVAR)]

    for r in range(2 * NVAR):
        state[r * SPACE : (r + 1) * SPACE] = arrived(r)
    place = lax.broadcasted_iota(jnp.int32, (SPACE, LANES), 0)
    hits = [(place == owner_ref[k, n]).astype(jnp.float32) for k in range(STEPS)]
    old_coarse = [restrict(arrived(2 * v), arrived(2 * v + 1)) for v in range(NVAR)]
    for k in range(STEPS):
        q, rates = fine_rate(state)
        scale = courant * hits[k]
        for v in range(NVAR):
            for i in range(2):
                at = slice((2 * v + i) * SPACE, (2 * v + i + 1) * SPACE)
                source = scale * arrived(2 * NVAR + 2 * v + i)
                first[at] = q[v][i] + rates[v][i] + source
        q1, rates1 = fine_rate(first)
        for v in range(NVAR):
            for i in range(2):
                at = slice((2 * v + i) * SPACE, (2 * v + i + 1) * SPACE)
                source = scale * arrived(2 * NVAR + 2 * v + i)
                state[at] = 0.5 * (state[at] + q1[v][i] + rates1[v][i] + source)

    final = [[state[(2 * v + i) * SPACE : (2 * v + i + 1) * SPACE] for i in range(2)] for v in range(NVAR)]
    count = hits[0] + hits[1] + hits[2]
    coarse_source = [
        courant * count * restrict(arrived(2 * NVAR + 2 * v), arrived(2 * NVAR + 2 * v + 1)) for v in range(NVAR)
    ]
    guess_old = [a + b for a, b in zip(coarse_advance(old_coarse), coarse_source)]
    for v in range(NVAR):
        gain = coarse_source[v] + restrict(final[v][0], final[v][1]) - guess_old[v]
        packed[8 * v : 8 * v + 8] = (
            gain[0:8] + turn(gain[8:16], 1) + turn(gain[16:24], 32) + turn(gain[24:32], 33)
        )

    def send_gain(k, c):
        pltpu.make_async_remote_copy(
            packed, gathered.at[n], send4.at[k], recv4.at[n], device_id={"cuts": n + k}, device_id_type=MESH
        ).start()
        return c

    def sent_gain(k, c):
        pltpu.make_async_remote_copy(
            packed, gathered.at[n], send4.at[k], recv4.at[n], device_id={"cuts": n + k}, device_id_type=MESH
        ).wait_send()
        return c

    lax.fori_loop(1, CUTS - n, send_gain, 0)

    for v in range(NVAR):
        for i in range(2):
            for j in range(4):
                out2[pl.ds(16 * 8 * j + 2 * v + i, 8, stride=16), :] = final[v][i][8 * j : 8 * j + 8]
    begin2, finish2 = exchange(out2, in2, 16, send2, recv2)
    begin2()

    useful = lane[8][0:8]

    def advance(m, c):
        pltpu.make_async_remote_copy(
            packed, gathered.at[m], send4.at[0], recv4.at[m], device_id={"cuts": m}, device_id_type=MESH
        ).wait_recv()
        moved = coarse_advance(list(c))
        result = []
        for v in range(NVAR):
            g = gathered[m, 8 * v : 8 * v + 8]
            parts = [useful * g, useful * turn(g, -1), useful * turn(g, -32), useful * turn(g, -33)]
            result.append(moved[v] + jnp.concatenate(parts, axis=0))
        return tuple(result)

    begin_coarse = []
    for v in range(NVAR):
        a = arrived(4 * NVAR + v // 2)
        begin_coarse.append(restrict_modes(turn(a, -1) if v % 2 else a))
    start = lax.fori_loop(0, n, advance, tuple(begin_coarse))
    guess_new = [a + b for a, b in zip(coarse_advance(list(start)), coarse_source)]
    for v in range(NVAR):
        change = guess_new[v] - guess_old[v]
        change = change + turn(change, 1)
        for j in range(4):
            out3[pl.ds(8 * 8 * j + v, 8, stride=8), :] = change[8 * j : 8 * j + 8]
    begin3, finish3 = exchange(out3, in3, 8, send3, recv3)
    begin3()

    finish2()
    halves = []
    for tile in range(2):
        rows = []
        for r in range(8):
            from_row = min(8 * tile + r, 2 * NVAR - 1)
            rows.append(
                jnp.concatenate([in2[pl.ds(16 * 8 * j + from_row, 8, stride=16), :] for j in range(4)], axis=0)
            )
        halves.append(jnp.concatenate(swap_blocks(rows), axis=0).T)
    modes = jnp.concatenate([halves[0], halves[1][: ROWS - LANES]], axis=0)
    fine[...] = jnp.dot(modes, forward_ref[...], precision=HIGHEST, preferred_element_type=jnp.float32)

    keep_fine = pltpu.make_async_copy(fine, fine_hbm, store.at[0])
    keep_fine.start()
    def to_next():
        return pltpu.make_async_remote_copy(
            fine, before_hbm, send5, recv5, device_id={"cuts": lax.rem(n + 1, CUTS)}, device_id_type=MESH
        )

    def keep_initial():
        return pltpu.make_async_copy(init_ref, before_hbm, store.at[2])

    @pl.when(n < CUTS - 1)
    def _():
        to_next().start()

    @pl.when(n == 0)
    def _():
        keep_initial().start()

    finish3()
    rows = []
    for v in range(8):
        from_row = min(v, NVAR - 1)
        rows.append(jnp.concatenate([in3[pl.ds(8 * 8 * j + from_row, 8, stride=8), :] for j in range(4)], axis=0))
    by_mode = swap_blocks(rows)
    change = jnp.concatenate([by_mode[0], by_mode[1], by_mode[4], by_mode[5]], axis=0).T
    change_ref[...] = jnp.dot(
        change[: NVAR * NY], back_ref[...], precision=HIGHEST, preferred_element_type=jnp.float32
    )
    keep_change = pltpu.make_async_copy(change_ref, change_hbm, store.at[1])
    keep_change.start()

    lax.fori_loop(1, CUTS - n, sent_gain, 0)
    keep_fine.wait()

    @pl.when(n > 0)
    def _():
        to_next().wait_recv()

    @pl.when(n < CUTS - 1)
    def _():
        to_next().wait_send()

    @pl.when(n == 0)
    def _():
        keep_initial().wait()

    keep_change.wait()


def body(old_starts, initial, blade_force, blade_owner):
    hbm = pl.BlockSpec(memory_space=pl.ANY)
    f32 = jnp.float32
    dma = pltpu.SemaphoreType.DMA
    fine, change, before = pl.pallas_call(
        kernel,
        out_shape=[jax.ShapeDtypeStruct((rows, NZ), f32) for rows in (ROWS, NVAR * NY, ROWS)],
        in_specs=[hbm] * 7,
        out_specs=[hbm] * 3,
        scratch_shapes=[
            pltpu.VMEM((ROWS, NZ), f32),
            pltpu.SMEM((STEPS, CUTS), jnp.int32),
            pltpu.VMEM((NZ, NZ), f32),
            pltpu.VMEM((NZ // 2, NZ), f32),
            pltpu.VMEM((16, LANES), f32),
            pltpu.VMEM((3 * LANES, NZ), f32),
            pltpu.VMEM((SPACE * 24, LANES), f32),
            pltpu.VMEM((SPACE * 24, LANES), f32),
            pltpu.VMEM((2 * NVAR * SPACE, LANES), f32),
            pltpu.VMEM((2 * NVAR * SPACE, LANES), f32),
            pltpu.VMEM((SPACE * 16, LANES), f32),
            pltpu.VMEM((SPACE * 16, LANES), f32),
            pltpu.VMEM((SPACE * 8, LANES), f32),
            pltpu.VMEM((SPACE * 8, LANES), f32),
            pltpu.VMEM((8 * NVAR, LANES), f32),
            pltpu.VMEM((CUTS, 8 * NVAR, LANES), f32),
            pltpu.VMEM((ROWS, NZ), f32),
            pltpu.VMEM((NVAR * NY, NZ), f32),
            dma((7,)),
            dma((SPACE,)),
            dma((SPACE,)),
            dma((SPACE,)),
            dma((SPACE,)),
            dma((SPACE,)),
            dma((SPACE,)),
            dma((CUTS,)),
            dma((CUTS,)),
            dma,
            dma,
            dma((3,)),
        ],
        compiler_params=pltpu.CompilerParams(
            collective_id=0, has_side_effects=True, vmem_limit_bytes=56 * 2**20
        ),
    )(
        old_starts.reshape(ROWS, NZ),
        initial.reshape(ROWS, NZ),
        blade_force.reshape(ROWS, NZ),
        blade_owner.T,
        jnp.asarray(FORWARD),
        jnp.asarray(BACK_COARSE),
        jnp.asarray(LANE_TABLE),
    )
    shape = old_starts.shape
    ends = fine.reshape(shape) + change.reshape(1, NVAR, 1, NY, NZ)
    return ends, old_starts - before.reshape(shape)


def solution(mesh):
    placed = (
        P("cuts", None, "space", None, None),
        P(None, "space", None, None),
        P(None, "space", None, None),
        P(),
    )
    return jax.shard_map(
        body,
        mesh=mesh,
        in_specs=placed,
        out_specs=(P("cuts", None, "space", None, None), P("cuts", None, "space", None, None)),
        check_vma=False,
    )
```

```python
import functools

import jax
import jax.numpy as jnp
import numpy as np
from jax import lax
from jax.experimental import pallas as pl
from jax.experimental.pallas import tpu as pltpu
from jax.sharding import PartitionSpec as P

MESH = pl.DeviceIdType.MESH
HIGHEST = lax.Precision.HIGHEST

STEPS = 3
NVAR = 5
NY = 16
NZ = 256
SPACE = 32
CUTS = 16
LANES = 128
ROWS = 2 * NVAR * NY

mach = 0.3
courant = 0.2
coarse_courant = 0.3


def wave(count, k, phase):
    angle = 2.0 * np.pi * k * np.arange(count) / count
    v = np.cos(angle) if phase == 0 else np.sin(angle)
    return v / np.sqrt(np.sum(v * v))


def group_waves(g):
    if g == 0:
        fine = [(0, 0), (64, 0), (128, 0), (64, 1)]
        coarse = [(0, 0), (64, 0)]
    else:
        fine = [(g, 0), (128 - g, 0), (g, 1), (128 - g, 1)]
        coarse = [(g, 0), (g, 1)]
    return fine, coarse


def make_tables():
    half = NZ // 2
    restrict_z = np.zeros((half, NZ))
    for j in range(half):
        restrict_z[j, 2 * j : 2 * j + 2] = 0.5
    forward = np.zeros((8, SPACE, NZ))
    back_coarse = np.zeros((4, SPACE, NZ))
    lanes = np.zeros((SPACE, 16, 8, NY))
    even = (np.arange(NY) % 2 == 0).astype(np.float64)
    for t in range(SPACE):
        for q in range(2):
            fine, coarse = group_waves(t + 32 * q)
            basis = [wave(NZ, *w) for w in fine]
            coarse_basis = [wave(half, *w) for w in coarse]
            for i in range(4):
                slot = q + 2 * i
                forward[slot, t] = basis[i]
                upper, lower = np.roll(basis[i], -1), np.roll(basis[i], 1)
                lanes[t, 0, slot] = basis[i] @ (upper + lower) - 2.0
                partner = basis[(i + 2) % 4]
                lanes[t, 1, slot] = basis[i] @ (np.roll(partner, -1) - np.roll(partner, 1))
            for i in range(2):
                slot = q + 4 * i
                back_coarse[q + 2 * i, t] = np.repeat(coarse_basis[i], 2)
                upper, lower = np.roll(coarse_basis[i], -1), np.roll(coarse_basis[i], 1)
                lanes[t, 2, slot] = coarse_basis[i] @ (upper + lower) - 2.0
                partner = coarse_basis[1 - i]
                lanes[t, 3, slot] = coarse_basis[i] @ (np.roll(partner, -1) - np.roll(partner, 1))
                for j in range(4):
                    source = (2 * i + j) % 4
                    lanes[t, 4 + j, slot] = 0.25 * (coarse_basis[i] @ (restrict_z @ basis[source])) * even
                lanes[t, 8, slot] = even
    return (
        forward.reshape(8 * SPACE, NZ).astype(np.float32),
        back_coarse.reshape(4 * SPACE, NZ).astype(np.float32),
        lanes.reshape(SPACE, 16, LANES).astype(np.float32),
    )


FORWARD, BACK_COARSE, LANE_TABLE = make_tables()
GATHER_ORDER = (12, 4, 11, 13, 3, 5, 10, 14, 2, 6, 9, 15, 1, 7, 8)


def in_two(a):
    high = a.astype(jnp.bfloat16)
    return high, (a - high.astype(jnp.float32)).astype(jnp.bfloat16)


def stack_table(a):
    high = a.astype(jnp.bfloat16)
    low = (a - high.astype(np.float32)).astype(jnp.bfloat16)
    return np.concatenate([high, high, low], axis=0)


def times_table(a, table):
    high, low = in_two(a)
    return jnp.dot(jnp.concatenate([high, low, high], axis=1), table, preferred_element_type=jnp.float32)


def turn(a, shift):
    return pltpu.roll(a, shift % LANES, 1)


def swap_blocks(arrays):
    arrays = list(arrays)
    block = lax.broadcasted_iota(jnp.int32, arrays[0].shape, 1) // NY
    for bit in (4, 2, 1):
        low = (block // bit) % 2 == 0
        for i in range(8):
            if i & bit == 0:
                a, b = arrays[i], arrays[i + bit]
                arrays[i] = jnp.where(low, a, turn(b, NY * bit))
                arrays[i + bit] = jnp.where(low, turn(a, -NY * bit), b)
    return arrays


def along_y(a, step):
    y = lax.broadcasted_iota(jnp.int32, a.shape, 1) % NY
    upper = jnp.where(y >= NY - step, turn(a, NY - step), turn(a, -step))
    lower = jnp.where(y < step, turn(a, step - NY), turn(a, step))
    return upper, lower


def below(a):
    row = lax.broadcasted_iota(jnp.int32, a.shape, 0)
    return jnp.where(row == 0, 0.0, pltpu.roll(a, 1, 0))


def above(a):
    row = lax.broadcasted_iota(jnp.int32, a.shape, 0)
    return jnp.where(row == a.shape[0] - 1, 0.0, pltpu.roll(a, a.shape[0] - 1, 0))


def rate_of(center, x_upper, x_lower, step, second_z, first_z, ratio):
    half = 0.5 * ratio
    own = second_z - 2.0 * (mach + 1.0) - 2.0
    rates = []
    ys = [along_y(center[v], step) for v in range(NVAR)]
    for v in range(NVAR):
        rates.append(x_upper[v] + (2.0 * mach + 1.0) * x_lower[v] + ys[v][0] + ys[v][1] + own * center[v])
    divergence = (x_upper[1] - x_lower[1]) + (ys[2][0] - ys[2][1]) + first_z * turn(center[3], 64)
    rates[0] = rates[0] - divergence
    rates[1] = rates[1] - (x_upper[4] - x_lower[4])
    rates[2] = rates[2] - (ys[4][0] - ys[4][1])
    rates[3] = rates[3] - first_z * turn(center[4], 64)
    rates[4] = rates[4] - divergence
    return [half * r for r in rates]


def kernel(
    old_hbm, init_hbm, force_hbm, owner_hbm, forward_hbm, inverse_hbm, back_hbm, table_hbm,
    ends_hbm, before_hbm,
    init_ref, owner_ref, forward_ref, inverse_ref, back_ref, table, stacked, out1, in1, state, first, out2, in2, out3, in3, packed, gathered, fine, ends,
    load, send1, recv1, send2, recv2, send3, recv3, send4, recv4, send5, recv5, store,
):
    n = lax.axis_index("cuts")
    s = lax.axis_index("space")

    def peer_of(k):
        return lax.rem(s + SPACE // 2 + (k // 2) * (1 - 2 * lax.rem(k, 2)), SPACE)

    old_ref = stacked.at[0:ROWS]
    loads = [
        pltpu.make_async_copy(source, target, load.at[i])
        for i, (source, target) in enumerate(
            (
                (forward_hbm, forward_ref),
                (old_hbm, old_ref),
                (force_hbm, stacked.at[ROWS : 2 * ROWS]),
                (init_hbm, init_ref),
                (owner_hbm, owner_ref),
                (table_hbm.at[s], table),
                (back_hbm, back_ref),
                (inverse_hbm, inverse_ref),
            )
        )
    ]
    for copy in loads:
        copy.start()

    barrier = pltpu.get_barrier_semaphore()

    def greet_space(k, c):
        pl.semaphore_signal(barrier, inc=1, device_id={"space": peer_of(k)}, device_id_type=MESH)
        return c

    def greet_cuts(k, c):
        pl.semaphore_signal(barrier, inc=1, device_id={"cuts": lax.rem(n + k, CUTS)}, device_id_type=MESH)
        return c

    lax.fori_loop(1, SPACE, greet_space, 0)
    lax.fori_loop(1, CUTS, greet_cuts, 0)

    for copy in loads[:4]:
        copy.wait()
    row = lax.broadcasted_iota(jnp.int32, (NY, NZ), 0)
    sums = []
    for v in range(NVAR):
        both = init_ref[2 * v * NY : (2 * v + 1) * NY] + init_ref[(2 * v + 1) * NY : (2 * v + 2) * NY]
        sums.append(both + pltpu.roll(both, NY - 1, 0))
    sums.append(jnp.zeros((NY, NZ), jnp.float32))
    for pair in range(3):
        merged = jnp.where(row % 2 == 0, sums[2 * pair], pltpu.roll(sums[2 * pair + 1], 1, 0))
        stacked[2 * ROWS + pair * NY : 2 * ROWS + (pair + 1) * NY] = merged
    stacked[2 * ROWS + 3 * NY :] = jnp.zeros((NY, NZ), jnp.float32)
    for tile in range(3):
        modes = lax.dot_general(
            forward_ref[...],
            stacked[tile * LANES : (tile + 1) * LANES],
            (((1,), (1,)), ((), ())),
            precision=HIGHEST,
            preferred_element_type=jnp.float32,
        )
        by_row = swap_blocks([modes[m * SPACE : (m + 1) * SPACE] for m in range(8)])
        for r in range(8):
            for j in range(4):
                out1[pl.ds(24 * 8 * j + 8 * tile + r, 8, stride=24), :] = by_row[r][8 * j : 8 * j + 8]

    pl.semaphore_wait(barrier, SPACE + CUTS - 2)

    def exchange(source, target, rows, send, recv):
        def piece(ref, i):
            if rows is None:
                return ref.at[i]
            return ref.at[pl.ds(pl.multiple_of(i * rows, 8), rows), :]

        def start(k, c):
            peer = peer_of(k)
            pltpu.make_async_remote_copy(
                piece(source, peer), piece(target, s), send, recv,
                device_id={"space": peer}, device_id_type=MESH,
            ).start()
            return c

        def begin():
            lax.fori_loop(1, SPACE, start, 0, unroll=True)
            if rows is None:
                target[s] = source[s]
            else:
                mine = pl.ds(pl.multiple_of(s * rows, 8), rows)
                target[mine, :] = source[mine, :]

        def finish():
            others = pl.ds(0, (SPACE - 1) * (rows or 1))
            pltpu.make_async_remote_copy(
                source.at[others], target.at[others], send, recv, device_id={"space": peer_of(1)}, device_id_type=MESH
            ).wait()

        return begin, finish

    begin1, finish1 = exchange(out1, in1, 24, send1, recv1)
    begin1()
    for copy in loads[4:]:
        copy.wait()
    finish1()

    lane = [jnp.broadcast_to(table[i : i + 1], (SPACE, LANES)) for i in range(9)]

    def arrived(r):
        return jnp.concatenate([in1[pl.ds(24 * 8 * j + r, 8, stride=24), :] for j in range(4)], axis=0)

    def restrict_modes(t):
        return lane[4] * t + lane[5] * turn(t, 96) + lane[6] * turn(t, 64) + lane[7] * turn(t, 32)

    def restrict(q0, q1):
        t = q0 + q1
        return restrict_modes(t + turn(t, -1))

    def fine_rate(ref):
        q = [[ref[(2 * v + i) * SPACE : (2 * v + i + 1) * SPACE] for i in range(2)] for v in range(NVAR)]
        low = rate_of(
            [q[v][0] for v in range(NVAR)], [q[v][1] for v in range(NVAR)], [below(q[v][1]) for v in range(NVAR)],
            1, lane[0], lane[1], courant,
        )
        high = rate_of(
            [q[v][1] for v in range(NVAR)], [above(q[v][0]) for v in range(NVAR)], [q[v][0] for v in range(NVAR)],
            1, lane[0], lane[1], courant,
        )
        return q, [[low[v], high[v]] for v in range(NVAR)]

    def coarse_advance(c):
        r = rate_of(c, [above(a) for a in c], [below(a) for a in c], 2, lane[2], lane[3], coarse_courant)
        return [c[v] + r[v] for v in range(NVAR)]

    for r in range(2 * NVAR):
        state[r * SPACE : (r + 1) * SPACE] = arrived(r)
    place = lax.broadcasted_iota(jnp.int32, (SPACE, LANES), 0)
    hits = [(place == owner_ref[k, n]).astype(jnp.float32) for k in range(STEPS)]
    old_coarse = [restrict(arrived(2 * v), arrived(2 * v + 1)) for v in range(NVAR)]
    for k in range(STEPS):
        q, rates = fine_rate(state)
        scale = courant * hits[k]
        for v in range(NVAR):
            for i in range(2):
                at = slice((2 * v + i) * SPACE, (2 * v + i + 1) * SPACE)
                source = scale * arrived(2 * NVAR + 2 * v + i)
                first[at] = q[v][i] + rates[v][i] + source
        q1, rates1 = fine_rate(first)
        for v in range(NVAR):
            for i in range(2):
                at = slice((2 * v + i) * SPACE, (2 * v + i + 1) * SPACE)
                source = scale * arrived(2 * NVAR + 2 * v + i)
                state[at] = 0.5 * (state[at] + q1[v][i] + rates1[v][i] + source)

    final = [[state[(2 * v + i) * SPACE : (2 * v + i + 1) * SPACE] for i in range(2)] for v in range(NVAR)]
    count = hits[0] + hits[1] + hits[2]
    coarse_source = [
        courant * count * restrict(arrived(2 * NVAR + 2 * v), arrived(2 * NVAR + 2 * v + 1)) for v in range(NVAR)
    ]
    guess_old = [a + b for a, b in zip(coarse_advance(old_coarse), coarse_source)]
    for v in range(NVAR):
        gain = coarse_source[v] + restrict(final[v][0], final[v][1]) - guess_old[v]
        packed[8 * v : 8 * v + 8] = (
            gain[0:8] + turn(gain[8:16], 1) + turn(gain[16:24], 32) + turn(gain[24:32], 33)
        )

    def send_gain(k):
        return pltpu.make_async_remote_copy(
            packed, gathered.at[n], send4.at[k], recv4.at[n], device_id={"cuts": n + k}, device_id_type=MESH
        )

    for k in GATHER_ORDER:
        @pl.when(n + k < CUTS)
        def _():
            send_gain(k).start()

    for v in range(NVAR):
        for i in range(2):
            out2[:, v, i, :] = final[v][i]
    begin2, finish2 = exchange(out2, in2, None, send2, recv2)
    begin2()

    useful = lane[8][0:8]

    def advance(m, c):
        pltpu.make_async_remote_copy(
            packed, gathered.at[m], send4.at[0], recv4.at[m], device_id={"cuts": m}, device_id_type=MESH
        ).wait_recv()
        moved = coarse_advance(list(c))
        result = []
        for v in range(NVAR):
            g = gathered[m, 8 * v : 8 * v + 8]
            parts = [useful * g, useful * turn(g, -1), useful * turn(g, -32), useful * turn(g, -33)]
            result.append(moved[v] + jnp.concatenate(parts, axis=0))
        return tuple(result)

    begin_coarse = []
    for v in range(NVAR):
        a = arrived(4 * NVAR + v // 2)
        begin_coarse.append(restrict_modes(turn(a, -1) if v % 2 else a))
    start = lax.fori_loop(0, n, advance, tuple(begin_coarse))
    guess_new = [a + b for a, b in zip(coarse_advance(list(start)), coarse_source)]
    change = [guess_new[v] - guess_old[v] for v in range(NVAR)]
    out3[:, 0, :] = change[0] + turn(change[1], 1) + turn(change[2], 32) + turn(change[3], 33)
    out3[:, 1, :] = change[4]
    begin3, finish3 = exchange(out3, in3, None, send3, recv3)
    begin3()

    finish2()
    halves = []
    for tile in range(2):
        rows = []
        for r in range(8):
            from_row = min(8 * tile + r, 2 * NVAR - 1)
            rows.append(in2[:, from_row // 2, from_row % 2, :])
        halves.append(jnp.concatenate(swap_blocks(rows), axis=0).T)
    modes = jnp.concatenate([halves[0], halves[1][: ROWS - LANES]], axis=0)
    fine[...] = times_table(modes, inverse_ref[...])

    def to_next():
        return pltpu.make_async_remote_copy(
            fine, before_hbm, send5, recv5, device_id={"cuts": lax.rem(n + 1, CUTS)}, device_id_type=MESH
        )

    def keep_initial():
        return pltpu.make_async_copy(init_ref, before_hbm, store.at[1])

    @pl.when(n < CUTS - 1)
    def _():
        to_next().start()

    @pl.when(n == 0)
    def _():
        keep_initial().start()

    finish3()
    mask = jnp.broadcast_to(useful[0:1], (SPACE, LANES))
    four = in3[:, 0, :]
    rows = [mask * a for a in (four, turn(four, -1), turn(four, -32), turn(four, -33))] + [in3[:, 1, :]]
    rows = [a + turn(a, 1) for a in rows]
    by_mode = swap_blocks(rows + rows[4:] * 3)
    change = jnp.concatenate([by_mode[0], by_mode[1], by_mode[4], by_mode[5]], axis=0).T
    change = times_table(change[: NVAR * NY], back_ref[...])
    for v in range(NVAR):
        for i in range(2):
            at = slice((2 * v + i) * NY, (2 * v + i + 1) * NY)
            ends[at] = fine[at] + change[v * NY : (v + 1) * NY]
    keep_ends = pltpu.make_async_copy(ends, ends_hbm, store.at[0])
    keep_ends.start()

    def sent_gain(k, c):
        send_gain(k).wait_send()
        return c

    lax.fori_loop(1, CUTS - n, sent_gain, 0)

    @pl.when(n > 0)
    def _():
        to_next().wait_recv()

    @pl.when(n < CUTS - 1)
    def _():
        to_next().wait_send()

    @pl.when(n == 0)
    def _():
        keep_initial().wait()

    keep_ends.wait()


def body(old_starts, initial, blade_force, blade_owner):
    hbm = pl.BlockSpec(memory_space=pl.ANY)
    f32 = jnp.float32
    dma = pltpu.SemaphoreType.DMA
    ends, before = pl.pallas_call(
        kernel,
        out_shape=[jax.ShapeDtypeStruct((rows, NZ), f32) for rows in (ROWS, ROWS)],
        in_specs=[hbm] * 8,
        out_specs=[hbm] * 2,
        scratch_shapes=[
            pltpu.VMEM((ROWS, NZ), f32),
            pltpu.SMEM((STEPS, CUTS), jnp.int32),
            pltpu.VMEM((NZ, NZ), f32),
            pltpu.VMEM((3 * NZ, NZ), jnp.bfloat16),
            pltpu.VMEM((3 * NZ // 2, NZ), jnp.bfloat16),
            pltpu.VMEM((16, LANES), f32),
            pltpu.VMEM((3 * LANES, NZ), f32),
            pltpu.VMEM((SPACE * 24, LANES), f32),
            pltpu.VMEM((SPACE * 24, LANES), f32),
            pltpu.VMEM((2 * NVAR * SPACE, LANES), f32),
            pltpu.VMEM((2 * NVAR * SPACE, LANES), f32),
            pltpu.VMEM((SPACE, NVAR, 2, LANES), f32),
            pltpu.VMEM((SPACE, NVAR, 2, LANES), f32),
            pltpu.VMEM((SPACE, 2, LANES), f32),
            pltpu.VMEM((SPACE, 2, LANES), f32),
            pltpu.VMEM((8 * NVAR, LANES), f32),
            pltpu.VMEM((CUTS, 8 * NVAR, LANES), f32),
            pltpu.VMEM((ROWS, NZ), f32),
            pltpu.VMEM((ROWS, NZ), f32),
            dma((8,)),
            dma,
            dma,
            dma,
            dma,
            dma,
            dma,
            dma((CUTS,)),
            dma((CUTS,)),
            dma,
            dma,
            dma((2,)),
        ],
        compiler_params=pltpu.CompilerParams(
            collective_id=0, has_side_effects=True, vmem_limit_bytes=56 * 2**20
        ),
    )(
        old_starts.reshape(ROWS, NZ),
        initial.reshape(ROWS, NZ),
        blade_force.reshape(ROWS, NZ),
        blade_owner.T,
        jnp.asarray(FORWARD),
        jnp.asarray(stack_table(FORWARD)),
        jnp.asarray(stack_table(BACK_COARSE)),
        jnp.asarray(LANE_TABLE),
    )
    shape = old_starts.shape
    return ends.reshape(shape), old_starts - before.reshape(shape)


def solution(mesh):
    placed = (
        P("cuts", None, "space", None, None),
        P(None, "space", None, None),
        P(None, "space", None, None),
        P(),
    )
    return jax.shard_map(
        body,
        mesh=mesh,
        in_specs=placed,
        out_specs=(P("cuts", None, "space", None, None), P("cuts", None, "space", None, None)),
        check_vma=False,
    )
```

```python
import functools

import jax
import jax.numpy as jnp
import numpy as np
from jax import lax
from jax.experimental import pallas as pl
from jax.experimental.pallas import tpu as pltpu
from jax.sharding import PartitionSpec as P

MESH = pl.DeviceIdType.MESH

STEPS = 3
NVAR = 5
NY = 16
NZ = 256
SPACE = 32
CUTS = 16
LANES = 128
ROWS = 2 * NVAR * NY

mach = 0.3
courant = 0.2
coarse_courant = 0.3


def wave(count, k, phase):
    angle = 2.0 * np.pi * k * np.arange(count) / count
    v = np.cos(angle) if phase == 0 else np.sin(angle)
    return v / np.sqrt(np.sum(v * v))


def group_waves(g):
    if g == 0:
        fine = [(0, 0), (64, 0), (128, 0), (64, 1)]
        coarse = [(0, 0), (64, 0)]
    else:
        fine = [(g, 0), (128 - g, 0), (g, 1), (128 - g, 1)]
        coarse = [(g, 0), (g, 1)]
    return fine, coarse


def make_tables():
    half = NZ // 2
    restrict_z = np.zeros((half, NZ))
    for j in range(half):
        restrict_z[j, 2 * j : 2 * j + 2] = 0.5
    forward = np.zeros((8, SPACE, NZ))
    back_coarse = np.zeros((4, SPACE, NZ))
    lanes = np.zeros((SPACE, 16, 8, NY))
    even = (np.arange(NY) % 2 == 0).astype(np.float64)
    for t in range(SPACE):
        for q in range(2):
            fine, coarse = group_waves(t + 32 * q)
            basis = [wave(NZ, *w) for w in fine]
            coarse_basis = [wave(half, *w) for w in coarse]
            for i in range(4):
                slot = q + 2 * i
                forward[slot, t] = basis[i]
                upper, lower = np.roll(basis[i], -1), np.roll(basis[i], 1)
                lanes[t, 0, slot] = basis[i] @ (upper + lower) - 2.0
                partner = basis[(i + 2) % 4]
                lanes[t, 1, slot] = basis[i] @ (np.roll(partner, -1) - np.roll(partner, 1))
            for i in range(2):
                slot = q + 4 * i
                back_coarse[q + 2 * i, t] = np.repeat(coarse_basis[i], 2)
                upper, lower = np.roll(coarse_basis[i], -1), np.roll(coarse_basis[i], 1)
                lanes[t, 2, slot] = coarse_basis[i] @ (upper + lower) - 2.0
                partner = coarse_basis[1 - i]
                lanes[t, 3, slot] = coarse_basis[i] @ (np.roll(partner, -1) - np.roll(partner, 1))
                for j in range(4):
                    source = (2 * i + j) % 4
                    lanes[t, 4 + j, slot] = 0.25 * (coarse_basis[i] @ (restrict_z @ basis[source])) * even
                lanes[t, 8, slot] = even
    return (
        forward.reshape(8 * SPACE, NZ).astype(np.float32),
        back_coarse.reshape(4 * SPACE, NZ).astype(np.float32),
        lanes.reshape(SPACE, 16, LANES).astype(np.float32),
    )


FORWARD, BACK_COARSE, LANE_TABLE = make_tables()
GATHER_ORDER = (12, 13, 11, 14, 10, 15, 9, 8, 7, 6, 5, 4, 3, 2, 1)


def in_two(a):
    high = a.astype(jnp.bfloat16)
    return high, (a - high.astype(jnp.float32)).astype(jnp.bfloat16)


def stack_table(a):
    high = a.astype(jnp.bfloat16)
    low = (a - high.astype(np.float32)).astype(jnp.bfloat16)
    return np.concatenate([high, high, low], axis=0)


def times_table(a, table):
    high, low = in_two(a)
    return jnp.dot(jnp.concatenate([high, low, high], axis=1), table, preferred_element_type=jnp.float32)


def turn(a, shift):
    return pltpu.roll(a, shift % LANES, 1)


def swap_blocks(arrays):
    arrays = list(arrays)
    block = lax.broadcasted_iota(jnp.int32, arrays[0].shape, 1) // NY
    for bit in (4, 2, 1):
        low = (block // bit) % 2 == 0
        for i in range(8):
            if i & bit == 0:
                a, b = arrays[i], arrays[i + bit]
                arrays[i] = jnp.where(low, a, turn(b, NY * bit))
                arrays[i + bit] = jnp.where(low, turn(a, -NY * bit), b)
    return arrays


def along_y(a, step):
    y = lax.broadcasted_iota(jnp.int32, a.shape, 1) % NY
    upper = jnp.where(y >= NY - step, turn(a, NY - step), turn(a, -step))
    lower = jnp.where(y < step, turn(a, step - NY), turn(a, step))
    return upper, lower


def below(a):
    row = lax.broadcasted_iota(jnp.int32, a.shape, 0)
    return jnp.where(row == 0, 0.0, pltpu.roll(a, 1, 0))


def above(a):
    row = lax.broadcasted_iota(jnp.int32, a.shape, 0)
    return jnp.where(row == a.shape[0] - 1, 0.0, pltpu.roll(a, a.shape[0] - 1, 0))


def rate_of(center, x_upper, x_lower, step, second_z, first_z, ratio):
    half = 0.5 * ratio
    own = second_z - 2.0 * (mach + 1.0) - 2.0
    rates = []
    ys = [along_y(center[v], step) for v in range(NVAR)]
    for v in range(NVAR):
        rates.append(x_upper[v] + (2.0 * mach + 1.0) * x_lower[v] + ys[v][0] + ys[v][1] + own * center[v])
    divergence = (x_upper[1] - x_lower[1]) + (ys[2][0] - ys[2][1]) + first_z * turn(center[3], 64)
    rates[0] = rates[0] - divergence
    rates[1] = rates[1] - (x_upper[4] - x_lower[4])
    rates[2] = rates[2] - (ys[4][0] - ys[4][1])
    rates[3] = rates[3] - first_z * turn(center[4], 64)
    rates[4] = rates[4] - divergence
    return [half * r for r in rates]


def kernel(
    old_hbm, init_hbm, force_hbm, owner_hbm, forward_hbm, inverse_hbm, back_hbm, table_hbm,
    ends_hbm, before_hbm,
    init_ref, owner_ref, forward_ref, inverse_ref, back_ref, table, stacked, out1, in1, state, first, out2, in2, out3, in3, out6, in6, packed, gathered, fine, ends,
    load, send1, recv1, send2, recv2, send3, recv3, send4, recv4, send5, recv5, send6, recv6, store,
):
    n = lax.axis_index("cuts")
    s = lax.axis_index("space")

    def peer_of(k):
        return lax.rem(s + SPACE // 2 + (k // 2) * (1 - 2 * lax.rem(k, 2)), SPACE)

    old_ref = stacked.at[0:ROWS]
    loads = [
        pltpu.make_async_copy(source, target, load.at[i])
        for i, (source, target) in enumerate(
            (
                (forward_hbm, forward_ref),
                (old_hbm, old_ref),
                (force_hbm, stacked.at[ROWS : 2 * ROWS]),
                (init_hbm, init_ref),
                (owner_hbm, owner_ref),
                (table_hbm.at[s], table),
                (back_hbm, back_ref),
                (inverse_hbm, inverse_ref),
            )
        )
    ]
    barrier = pltpu.get_barrier_semaphore()

    def greet_space(k, c):
        pl.semaphore_signal(barrier, inc=1, device_id={"space": peer_of(k)}, device_id_type=MESH)
        return c

    def greet_cuts(k, c):
        pl.semaphore_signal(barrier, inc=1, device_id={"cuts": lax.rem(n + k, CUTS)}, device_id_type=MESH)
        return c

    lax.fori_loop(1, SPACE, greet_space, 0, unroll=True)
    lax.fori_loop(1, CUTS, greet_cuts, 0, unroll=True)

    for copy in loads:
        copy.start()

    for copy in loads[:4]:
        copy.wait()
    row = lax.broadcasted_iota(jnp.int32, (NY, NZ), 0)
    sums = []
    for v in range(NVAR):
        both = init_ref[2 * v * NY : (2 * v + 1) * NY] + init_ref[(2 * v + 1) * NY : (2 * v + 2) * NY]
        sums.append(both + pltpu.roll(both, NY - 1, 0))
    sums.append(jnp.zeros((NY, NZ), jnp.float32))
    for pair in range(3):
        merged = jnp.where(row % 2 == 0, sums[2 * pair], pltpu.roll(sums[2 * pair + 1], 1, 0))
        stacked[2 * ROWS + pair * NY : 2 * ROWS + (pair + 1) * NY] = merged
    stacked[2 * ROWS + 3 * NY :] = jnp.zeros((NY, NZ), jnp.float32)
    for tile in range(3):
        high, low = in_two(stacked[tile * LANES : (tile + 1) * LANES])
        modes = lax.dot_general(
            forward_ref[...],
            jnp.concatenate([high, low, high], axis=1),
            (((1,), (1,)), ((), ())),
            preferred_element_type=jnp.float32,
        )
        by_row = swap_blocks([modes[m * SPACE : (m + 1) * SPACE] for m in range(8)])
        for r in range(8):
            at = 8 * tile + r
            if at < 4 * NVAR:
                out1[:, at // 2, at % 2, :] = by_row[r]
            else:
                out6[:, at // 2 - 2 * NVAR, at % 2, :] = by_row[r]

    pl.semaphore_wait(barrier, SPACE + CUTS - 2)

    def exchange(source, target, send, recv):
        def start(k, c):
            peer = peer_of(k)
            pltpu.make_async_remote_copy(
                source.at[peer], target.at[s], send, recv, device_id={"space": peer}, device_id_type=MESH
            ).start()
            return c

        def begin():
            lax.fori_loop(1, SPACE, start, 0, unroll=True)
            target[s] = source[s]

        def finish():
            others = pl.ds(0, SPACE - 1)
            pltpu.make_async_remote_copy(
                source.at[others], target.at[others], send, recv, device_id={"space": peer_of(1)}, device_id_type=MESH
            ).wait()

        return begin, finish

    begin1, finish1 = exchange(out1, in1, send1, recv1)
    begin6, finish6 = exchange(out6, in6, send6, recv6)
    begin1()
    begin6()
    for copy in loads[4:]:
        copy.wait()
    finish1()

    lane = [jnp.broadcast_to(table[i : i + 1], (SPACE, LANES)) for i in range(9)]

    def arrived(r):
        if r < 4 * NVAR:
            return in1[:, r // 2, r % 2, :]
        return in6[:, r // 2 - 2 * NVAR, r % 2, :]

    def restrict_modes(t):
        return lane[4] * t + lane[5] * turn(t, 96) + lane[6] * turn(t, 64) + lane[7] * turn(t, 32)

    def restrict(q0, q1):
        t = q0 + q1
        return restrict_modes(t + turn(t, -1))

    def fine_rate(ref):
        q = [[ref[(2 * v + i) * SPACE : (2 * v + i + 1) * SPACE] for i in range(2)] for v in range(NVAR)]
        low = rate_of(
            [q[v][0] for v in range(NVAR)], [q[v][1] for v in range(NVAR)], [below(q[v][1]) for v in range(NVAR)],
            1, lane[0], lane[1], courant,
        )
        high = rate_of(
            [q[v][1] for v in range(NVAR)], [above(q[v][0]) for v in range(NVAR)], [q[v][0] for v in range(NVAR)],
            1, lane[0], lane[1], courant,
        )
        return q, [[low[v], high[v]] for v in range(NVAR)]

    def coarse_advance(c):
        r = rate_of(c, [above(a) for a in c], [below(a) for a in c], 2, lane[2], lane[3], coarse_courant)
        return [c[v] + r[v] for v in range(NVAR)]

    for r in range(2 * NVAR):
        state[r * SPACE : (r + 1) * SPACE] = arrived(r)
    place = lax.broadcasted_iota(jnp.int32, (SPACE, LANES), 0)
    hits = [(place == owner_ref[k, n]).astype(jnp.float32) for k in range(STEPS)]
    old_coarse = [restrict(arrived(2 * v), arrived(2 * v + 1)) for v in range(NVAR)]
    for k in range(STEPS):
        q, rates = fine_rate(state)
        scale = courant * hits[k]
        for v in range(NVAR):
            for i in range(2):
                at = slice((2 * v + i) * SPACE, (2 * v + i + 1) * SPACE)
                source = scale * arrived(2 * NVAR + 2 * v + i)
                first[at] = q[v][i] + rates[v][i] + source
        q1, rates1 = fine_rate(first)
        for v in range(NVAR):
            for i in range(2):
                at = slice((2 * v + i) * SPACE, (2 * v + i + 1) * SPACE)
                source = scale * arrived(2 * NVAR + 2 * v + i)
                state[at] = 0.5 * (state[at] + q1[v][i] + rates1[v][i] + source)

    final = [[state[(2 * v + i) * SPACE : (2 * v + i + 1) * SPACE] for i in range(2)] for v in range(NVAR)]
    count = hits[0] + hits[1] + hits[2]
    coarse_source = [
        courant * count * restrict(arrived(2 * NVAR + 2 * v), arrived(2 * NVAR + 2 * v + 1)) for v in range(NVAR)
    ]
    guess_old = [a + b for a, b in zip(coarse_advance(old_coarse), coarse_source)]
    for v in range(NVAR):
        gain = coarse_source[v] + restrict(final[v][0], final[v][1]) - guess_old[v]
        packed[8 * v : 8 * v + 8] = (
            gain[0:8] + turn(gain[8:16], 1) + turn(gain[16:24], 32) + turn(gain[24:32], 33)
        )

    def send_gain(k):
        return pltpu.make_async_remote_copy(
            packed, gathered.at[n], send4.at[k], recv4.at[n], device_id={"cuts": n + k}, device_id_type=MESH
        )

    for k in GATHER_ORDER:
        @pl.when(n + k < CUTS)
        def _():
            send_gain(k).start()

    for v in range(NVAR):
        for i in range(2):
            out2[:, v, i, :] = final[v][i]
    begin2, finish2 = exchange(out2, in2, send2, recv2)
    begin2()

    useful = lane[8][0:8]

    def advance(m, c):
        pltpu.make_async_remote_copy(
            packed, gathered.at[m], send4.at[0], recv4.at[m], device_id={"cuts": m}, device_id_type=MESH
        ).wait_recv()
        moved = coarse_advance(list(c))
        result = []
        for v in range(NVAR):
            g = gathered[m, 8 * v : 8 * v + 8]
            parts = [useful * g, useful * turn(g, -1), useful * turn(g, -32), useful * turn(g, -33)]
            result.append(moved[v] + jnp.concatenate(parts, axis=0))
        return tuple(result)

    finish6()
    begin_coarse = []
    for v in range(NVAR):
        a = arrived(4 * NVAR + v // 2)
        begin_coarse.append(restrict_modes(turn(a, -1) if v % 2 else a))
    start = lax.fori_loop(0, n, advance, tuple(begin_coarse))
    guess_new = [a + b for a, b in zip(coarse_advance(list(start)), coarse_source)]
    change = [guess_new[v] - guess_old[v] for v in range(NVAR)]
    out3[:, 0, :] = change[0] + turn(change[1], 1) + turn(change[2], 32) + turn(change[3], 33)
    out3[:, 1, :] = change[4]
    begin3, finish3 = exchange(out3, in3, send3, recv3)
    begin3()

    finish2()
    halves = []
    for tile in range(2):
        rows = []
        for r in range(8):
            from_row = min(8 * tile + r, 2 * NVAR - 1)
            rows.append(in2[:, from_row // 2, from_row % 2, :])
        halves.append(jnp.concatenate(swap_blocks(rows), axis=0).T)
    modes = jnp.concatenate([halves[0], halves[1][: ROWS - LANES]], axis=0)
    fine[...] = times_table(modes, inverse_ref[...])

    def to_next():
        return pltpu.make_async_remote_copy(
            fine, before_hbm, send5, recv5, device_id={"cuts": lax.rem(n + 1, CUTS)}, device_id_type=MESH
        )

    def keep_initial():
        return pltpu.make_async_copy(init_ref, before_hbm, store.at[1])

    @pl.when(n < CUTS - 1)
    def _():
        to_next().start()

    @pl.when(n == 0)
    def _():
        keep_initial().start()

    finish3()
    mask = jnp.broadcast_to(useful[0:1], (SPACE, LANES))
    four = in3[:, 0, :]
    rows = [mask * a for a in (four, turn(four, -1), turn(four, -32), turn(four, -33))] + [in3[:, 1, :]]
    rows = [a + turn(a, 1) for a in rows]
    by_mode = swap_blocks(rows + rows[4:] * 3)
    change = jnp.concatenate([by_mode[0], by_mode[1], by_mode[4], by_mode[5]], axis=0).T
    change = times_table(change[: NVAR * NY], back_ref[...])
    for v in range(NVAR):
        for i in range(2):
            at = slice((2 * v + i) * NY, (2 * v + i + 1) * NY)
            ends[at] = fine[at] + change[v * NY : (v + 1) * NY]
    keep_ends = pltpu.make_async_copy(ends, ends_hbm, store.at[0])
    keep_ends.start()

    def sent_gain(k, c):
        send_gain(k).wait_send()
        return c

    lax.fori_loop(1, CUTS - n, sent_gain, 0)

    @pl.when(n > 0)
    def _():
        to_next().wait_recv()

    @pl.when(n < CUTS - 1)
    def _():
        to_next().wait_send()

    @pl.when(n == 0)
    def _():
        keep_initial().wait()

    keep_ends.wait()


def body(old_starts, initial, blade_force, blade_owner):
    hbm = pl.BlockSpec(memory_space=pl.ANY)
    f32 = jnp.float32
    dma = pltpu.SemaphoreType.DMA
    ends, before = pl.pallas_call(
        kernel,
        out_shape=[jax.ShapeDtypeStruct((rows, NZ), f32) for rows in (ROWS, ROWS)],
        in_specs=[hbm] * 8,
        out_specs=[hbm] * 2,
        scratch_shapes=[
            pltpu.VMEM((ROWS, NZ), f32),
            pltpu.SMEM((STEPS, CUTS), jnp.int32),
            pltpu.VMEM((NZ, 3 * NZ), jnp.bfloat16),
            pltpu.VMEM((3 * NZ, NZ), jnp.bfloat16),
            pltpu.VMEM((3 * NZ // 2, NZ), jnp.bfloat16),
            pltpu.VMEM((16, LANES), f32),
            pltpu.VMEM((3 * LANES, NZ), f32),
            pltpu.VMEM((SPACE, 2 * NVAR, 2, LANES), f32),
            pltpu.VMEM((SPACE, 2 * NVAR, 2, LANES), f32),
            pltpu.VMEM((2 * NVAR * SPACE, LANES), f32),
            pltpu.VMEM((2 * NVAR * SPACE, LANES), f32),
            pltpu.VMEM((SPACE, NVAR, 2, LANES), f32),
            pltpu.VMEM((SPACE, NVAR, 2, LANES), f32),
            pltpu.VMEM((SPACE, 2, LANES), f32),
            pltpu.VMEM((SPACE, 2, LANES), f32),
            pltpu.VMEM((SPACE, 2, 2, LANES), f32),
            pltpu.VMEM((SPACE, 2, 2, LANES), f32),
            pltpu.VMEM((8 * NVAR, LANES), f32),
            pltpu.VMEM((CUTS, 8 * NVAR, LANES), f32),
            pltpu.VMEM((ROWS, NZ), f32),
            pltpu.VMEM((ROWS, NZ), f32),
            dma((8,)),
            dma,
            dma,
            dma,
            dma,
            dma,
            dma,
            dma((CUTS,)),
            dma((CUTS,)),
            dma,
            dma,
            dma,
            dma,
            dma((2,)),
        ],
        compiler_params=pltpu.CompilerParams(
            collective_id=0, has_side_effects=True, vmem_limit_bytes=56 * 2**20
        ),
    )(
        old_starts.reshape(ROWS, NZ),
        initial.reshape(ROWS, NZ),
        blade_force.reshape(ROWS, NZ),
        blade_owner.T,
        jnp.asarray(np.ascontiguousarray(stack_table(FORWARD.T).T)),
        jnp.asarray(stack_table(FORWARD)),
        jnp.asarray(stack_table(BACK_COARSE)),
        jnp.asarray(LANE_TABLE),
    )
    shape = old_starts.shape
    return ends.reshape(shape), old_starts - before.reshape(shape)


def solution(mesh):
    placed = (
        P("cuts", None, "space", None, None),
        P(None, "space", None, None),
        P(None, "space", None, None),
        P(),
    )
    return jax.shard_map(
        body,
        mesh=mesh,
        in_specs=placed,
        out_specs=(P("cuts", None, "space", None, None), P("cuts", None, "space", None, None)),
        check_vma=False,
    )
```

```python
import functools

import jax
import jax.numpy as jnp
import numpy as np
from jax import lax
from jax.experimental import pallas as pl
from jax.experimental.pallas import tpu as pltpu
from jax.sharding import PartitionSpec as P

MESH = pl.DeviceIdType.MESH

STEPS = 3
NVAR = 5
NY = 16
NZ = 256
SPACE = 32
CUTS = 16
LANES = 128
ROWS = 2 * NVAR * NY

mach = 0.3
courant = 0.2
coarse_courant = 0.3


def wave(count, k, phase):
    angle = 2.0 * np.pi * k * np.arange(count) / count
    v = np.cos(angle) if phase == 0 else np.sin(angle)
    return v / np.sqrt(np.sum(v * v))


def group_waves(g):
    if g == 0:
        fine = [(0, 0), (64, 0), (128, 0), (64, 1)]
        coarse = [(0, 0), (64, 0)]
    else:
        fine = [(g, 0), (128 - g, 0), (g, 1), (128 - g, 1)]
        coarse = [(g, 0), (g, 1)]
    return fine, coarse


def make_tables():
    half = NZ // 2
    restrict_z = np.zeros((half, NZ))
    for j in range(half):
        restrict_z[j, 2 * j : 2 * j + 2] = 0.5
    forward = np.zeros((8, SPACE, NZ))
    back_coarse = np.zeros((4, SPACE, NZ))
    lanes = np.zeros((SPACE, 16, 8, NY))
    even = (np.arange(NY) % 2 == 0).astype(np.float64)
    for t in range(SPACE):
        for q in range(2):
            fine, coarse = group_waves(t + 32 * q)
            basis = [wave(NZ, *w) for w in fine]
            coarse_basis = [wave(half, *w) for w in coarse]
            for i in range(4):
                slot = q + 2 * i
                forward[slot, t] = basis[i]
                upper, lower = np.roll(basis[i], -1), np.roll(basis[i], 1)
                lanes[t, 0, slot] = basis[i] @ (upper + lower) - 2.0
                partner = basis[(i + 2) % 4]
                lanes[t, 1, slot] = basis[i] @ (np.roll(partner, -1) - np.roll(partner, 1))
            for i in range(2):
                slot = q + 4 * i
                back_coarse[q + 2 * i, t] = np.repeat(coarse_basis[i], 2)
                upper, lower = np.roll(coarse_basis[i], -1), np.roll(coarse_basis[i], 1)
                lanes[t, 2, slot] = coarse_basis[i] @ (upper + lower) - 2.0
                partner = coarse_basis[1 - i]
                lanes[t, 3, slot] = coarse_basis[i] @ (np.roll(partner, -1) - np.roll(partner, 1))
                for j in range(4):
                    source = (2 * i + j) % 4
                    lanes[t, 4 + j, slot] = 0.25 * (coarse_basis[i] @ (restrict_z @ basis[source])) * even
                lanes[t, 8, slot] = even
    return (
        forward.reshape(8 * SPACE, NZ).astype(np.float32),
        back_coarse.reshape(4 * SPACE, NZ).astype(np.float32),
        lanes.reshape(SPACE, 16, LANES).astype(np.float32),
    )


FORWARD, BACK_COARSE, LANE_TABLE = make_tables()
GATHER_ORDER = (12, 13, 11, 14, 10, 15, 9, 8, 7, 6, 5, 4, 3, 2, 1)


def in_two(a):
    high = a.astype(jnp.bfloat16)
    return high, (a - high.astype(jnp.float32)).astype(jnp.bfloat16)


def stack_table(a):
    high = a.astype(jnp.bfloat16)
    low = (a - high.astype(np.float32)).astype(jnp.bfloat16)
    return np.concatenate([high, high, low], axis=0)


def times_table(a, table):
    high, low = in_two(a)
    return jnp.dot(jnp.concatenate([high, low, high], axis=1), table, preferred_element_type=jnp.float32)


def turn(a, shift):
    return pltpu.roll(a, shift % LANES, 1)


def swap_blocks(arrays):
    arrays = list(arrays)
    block = lax.broadcasted_iota(jnp.int32, arrays[0].shape, 1) // NY
    for bit in (4, 2, 1):
        low = (block // bit) % 2 == 0
        for i in range(8):
            if i & bit == 0:
                a, b = arrays[i], arrays[i + bit]
                arrays[i] = jnp.where(low, a, turn(b, NY * bit))
                arrays[i + bit] = jnp.where(low, turn(a, -NY * bit), b)
    return arrays


def along_y(a, step):
    y = lax.broadcasted_iota(jnp.int32, a.shape, 1) % NY
    upper = jnp.where(y >= NY - step, turn(a, NY - step), turn(a, -step))
    lower = jnp.where(y < step, turn(a, step - NY), turn(a, step))
    return upper, lower


def below(a):
    row = lax.broadcasted_iota(jnp.int32, a.shape, 0)
    return jnp.where(row == 0, 0.0, pltpu.roll(a, 1, 0))


def above(a):
    row = lax.broadcasted_iota(jnp.int32, a.shape, 0)
    return jnp.where(row == a.shape[0] - 1, 0.0, pltpu.roll(a, a.shape[0] - 1, 0))


def rate_of(center, x_upper, x_lower, step, second_z, first_z, ratio):
    half = 0.5 * ratio
    own = second_z - 2.0 * (mach + 1.0) - 2.0
    rates = []
    ys = [along_y(center[v], step) for v in range(NVAR)]
    for v in range(NVAR):
        rates.append(x_upper[v] + (2.0 * mach + 1.0) * x_lower[v] + ys[v][0] + ys[v][1] + own * center[v])
    divergence = (x_upper[1] - x_lower[1]) + (ys[2][0] - ys[2][1]) + first_z * turn(center[3], 64)
    rates[0] = rates[0] - divergence
    rates[1] = rates[1] - (x_upper[4] - x_lower[4])
    rates[2] = rates[2] - (ys[4][0] - ys[4][1])
    rates[3] = rates[3] - first_z * turn(center[4], 64)
    rates[4] = rates[4] - divergence
    return [half * r for r in rates]


def kernel(
    old_hbm, init_hbm, force_hbm, owner_hbm, forward_hbm, inverse_hbm, back_hbm, table_hbm,
    ends, before_hbm,
    init_ref, owner_ref, forward_ref, inverse_ref, back_ref, table, stacked, out1, in1, state, first, out2, in2, out3, in3, out6, in6, packed, gathered, fine,
    load, send1, recv1, send2, recv2, send3, recv3, send4, recv4, send5, recv5, send6, recv6, store,
):
    n = lax.axis_index("cuts")
    s = lax.axis_index("space")

    def peer_of(k):
        return lax.rem(s + SPACE // 2 + (k // 2) * (1 - 2 * lax.rem(k, 2)), SPACE)

    old_ref = stacked.at[0:ROWS]
    loads = [
        pltpu.make_async_copy(source, target, load.at[i])
        for i, (source, target) in enumerate(
            (
                (forward_hbm, forward_ref),
                (old_hbm, old_ref),
                (force_hbm, stacked.at[ROWS : 2 * ROWS]),
                (init_hbm, init_ref),
                (owner_hbm, owner_ref),
                (table_hbm.at[s], table),
                (back_hbm, back_ref),
                (inverse_hbm, inverse_ref),
            )
        )
    ]
    barrier = pltpu.get_barrier_semaphore()

    def greet_space(k, c):
        pl.semaphore_signal(barrier, inc=1, device_id={"space": peer_of(k)}, device_id_type=MESH)
        return c

    def greet_cuts(k, c):
        pl.semaphore_signal(barrier, inc=1, device_id={"cuts": n - k}, device_id_type=MESH)
        return c

    lax.fori_loop(1, SPACE, greet_space, 0, unroll=True)
    lax.fori_loop(1, n + 1, greet_cuts, 0)

    for copy in loads:
        copy.start()

    for copy in loads[:4]:
        copy.wait()
    row = lax.broadcasted_iota(jnp.int32, (NY, NZ), 0)
    sums = []
    for v in range(NVAR):
        both = init_ref[2 * v * NY : (2 * v + 1) * NY] + init_ref[(2 * v + 1) * NY : (2 * v + 2) * NY]
        sums.append(both + pltpu.roll(both, NY - 1, 0))
    sums.append(jnp.zeros((NY, NZ), jnp.float32))
    for pair in range(3):
        merged = jnp.where(row % 2 == 0, sums[2 * pair], pltpu.roll(sums[2 * pair + 1], 1, 0))
        stacked[2 * ROWS + pair * NY : 2 * ROWS + (pair + 1) * NY] = merged
    stacked[2 * ROWS + 3 * NY :] = jnp.zeros((NY, NZ), jnp.float32)
    for tile in range(3):
        high, low = in_two(stacked[tile * LANES : (tile + 1) * LANES])
        modes = lax.dot_general(
            forward_ref[...],
            jnp.concatenate([high, low, high], axis=1),
            (((1,), (1,)), ((), ())),
            preferred_element_type=jnp.float32,
        )
        by_row = swap_blocks([modes[m * SPACE : (m + 1) * SPACE] for m in range(8)])
        for r in range(8):
            at = 8 * tile + r
            if at < 4 * NVAR:
                out1[:, at // 2, at % 2, :] = by_row[r]
            else:
                out6[:, at // 2 - 2 * NVAR, at % 2, :] = by_row[r]

    pl.semaphore_wait(barrier, SPACE - 1 + CUTS - 1 - n)

    def exchange(source, target, send, recv):
        def start(k, c):
            peer = peer_of(k)
            pltpu.make_async_remote_copy(
                source.at[peer], target.at[s], send, recv, device_id={"space": peer}, device_id_type=MESH
            ).start()
            return c

        def begin():
            lax.fori_loop(1, SPACE, start, 0, unroll=True)
            target[s] = source[s]

        def finish():
            others = pl.ds(0, SPACE - 1)
            pltpu.make_async_remote_copy(
                source.at[others], target.at[others], send, recv, device_id={"space": peer_of(1)}, device_id_type=MESH
            ).wait()

        return begin, finish

    begin1, finish1 = exchange(out1, in1, send1, recv1)
    begin6, finish6 = exchange(out6, in6, send6, recv6)
    begin1()
    begin6()
    for copy in loads[4:]:
        copy.wait()
    finish1()

    lane = [jnp.broadcast_to(table[i : i + 1], (SPACE, LANES)) for i in range(9)]

    def arrived(r):
        if r < 4 * NVAR:
            return in1[:, r // 2, r % 2, :]
        return in6[:, r // 2 - 2 * NVAR, r % 2, :]

    def restrict_modes(t):
        return lane[4] * t + lane[5] * turn(t, 96) + lane[6] * turn(t, 64) + lane[7] * turn(t, 32)

    def restrict(q0, q1):
        t = q0 + q1
        return restrict_modes(t + turn(t, -1))

    def fine_rate(ref):
        q = [[ref[(2 * v + i) * SPACE : (2 * v + i + 1) * SPACE] for i in range(2)] for v in range(NVAR)]
        low = rate_of(
            [q[v][0] for v in range(NVAR)], [q[v][1] for v in range(NVAR)], [below(q[v][1]) for v in range(NVAR)],
            1, lane[0], lane[1], courant,
        )
        high = rate_of(
            [q[v][1] for v in range(NVAR)], [above(q[v][0]) for v in range(NVAR)], [q[v][0] for v in range(NVAR)],
            1, lane[0], lane[1], courant,
        )
        return q, [[low[v], high[v]] for v in range(NVAR)]

    def coarse_advance(c):
        r = rate_of(c, [above(a) for a in c], [below(a) for a in c], 2, lane[2], lane[3], coarse_courant)
        return [c[v] + r[v] for v in range(NVAR)]

    for r in range(2 * NVAR):
        state[r * SPACE : (r + 1) * SPACE] = arrived(r)
    place = lax.broadcasted_iota(jnp.int32, (SPACE, LANES), 0)
    hits = [(place == owner_ref[k, n]).astype(jnp.float32) for k in range(STEPS)]
    old_coarse = [restrict(arrived(2 * v), arrived(2 * v + 1)) for v in range(NVAR)]
    for k in range(STEPS):
        q, rates = fine_rate(state)
        scale = courant * hits[k]
        for v in range(NVAR):
            for i in range(2):
                at = slice((2 * v + i) * SPACE, (2 * v + i + 1) * SPACE)
                source = scale * arrived(2 * NVAR + 2 * v + i)
                first[at] = q[v][i] + rates[v][i] + source
        q1, rates1 = fine_rate(first)
        for v in range(NVAR):
            for i in range(2):
                at = slice((2 * v + i) * SPACE, (2 * v + i + 1) * SPACE)
                source = scale * arrived(2 * NVAR + 2 * v + i)
                state[at] = 0.5 * (state[at] + q1[v][i] + rates1[v][i] + source)

    final = [[state[(2 * v + i) * SPACE : (2 * v + i + 1) * SPACE] for i in range(2)] for v in range(NVAR)]
    count = hits[0] + hits[1] + hits[2]
    coarse_source = [
        courant * count * restrict(arrived(2 * NVAR + 2 * v), arrived(2 * NVAR + 2 * v + 1)) for v in range(NVAR)
    ]
    guess_old = [a + b for a, b in zip(coarse_advance(old_coarse), coarse_source)]
    for v in range(NVAR):
        gain = coarse_source[v] + restrict(final[v][0], final[v][1]) - guess_old[v]
        packed[8 * v : 8 * v + 8] = (
            gain[0:8] + turn(gain[8:16], 1) + turn(gain[16:24], 32) + turn(gain[24:32], 33)
        )

    def send_gain(k):
        return pltpu.make_async_remote_copy(
            packed, gathered.at[n], send4.at[k], recv4.at[n], device_id={"cuts": n + k}, device_id_type=MESH
        )

    for k in GATHER_ORDER:
        @pl.when(n + k < CUTS)
        def _():
            send_gain(k).start()

    for v in range(NVAR):
        for i in range(2):
            out2[:, v, i, :] = final[v][i]
    begin2, finish2 = exchange(out2, in2, send2, recv2)
    begin2()

    useful = lane[8][0:8]

    def advance(m, c):
        pltpu.make_async_remote_copy(
            packed, gathered.at[m], send4.at[0], recv4.at[m], device_id={"cuts": m}, device_id_type=MESH
        ).wait_recv()
        moved = coarse_advance(list(c))
        result = []
        for v in range(NVAR):
            g = gathered[m, 8 * v : 8 * v + 8]
            parts = [useful * g, useful * turn(g, -1), useful * turn(g, -32), useful * turn(g, -33)]
            result.append(moved[v] + jnp.concatenate(parts, axis=0))
        return tuple(result)

    finish6()
    begin_coarse = []
    for v in range(NVAR):
        a = arrived(4 * NVAR + v // 2)
        begin_coarse.append(restrict_modes(turn(a, -1) if v % 2 else a))
    start = lax.fori_loop(0, n, advance, tuple(begin_coarse))
    guess_new = [a + b for a, b in zip(coarse_advance(list(start)), coarse_source)]
    change = [guess_new[v] - guess_old[v] for v in range(NVAR)]
    out3[:, 0, :] = change[0] + turn(change[1], 1) + turn(change[2], 32) + turn(change[3], 33)
    out3[:, 1, :] = change[4]
    begin3, finish3 = exchange(out3, in3, send3, recv3)
    begin3()

    finish2()
    halves = []
    for tile in range(2):
        rows = []
        for r in range(8):
            from_row = min(8 * tile + r, 2 * NVAR - 1)
            rows.append(in2[:, from_row // 2, from_row % 2, :])
        halves.append(jnp.concatenate(swap_blocks(rows), axis=0).T)
    modes = jnp.concatenate([halves[0], halves[1][: ROWS - LANES]], axis=0)
    fine[...] = times_table(modes, inverse_ref[...])

    def to_next():
        return pltpu.make_async_remote_copy(
            fine, before_hbm, send5, recv5, device_id={"cuts": lax.rem(n + 1, CUTS)}, device_id_type=MESH
        )

    def keep_initial():
        return pltpu.make_async_copy(init_ref, before_hbm, store)

    @pl.when(n < CUTS - 1)
    def _():
        to_next().start()

    @pl.when(n == 0)
    def _():
        keep_initial().start()

    finish3()
    mask = jnp.broadcast_to(useful[0:1], (SPACE, LANES))
    four = in3[:, 0, :]
    rows = [mask * a for a in (four, turn(four, -1), turn(four, -32), turn(four, -33))] + [in3[:, 1, :]]
    rows = [a + turn(a, 1) for a in rows]
    by_mode = swap_blocks(rows + rows[4:] * 3)
    change = jnp.concatenate([by_mode[0], by_mode[1], by_mode[4], by_mode[5]], axis=0).T
    change = times_table(change[: NVAR * NY], back_ref[...])
    for v in range(NVAR):
        for i in range(2):
            at = slice((2 * v + i) * NY, (2 * v + i + 1) * NY)
            ends[at] = fine[at] + change[v * NY : (v + 1) * NY]
    def sent_gain(k, c):
        send_gain(k).wait_send()
        return c

    lax.fori_loop(1, CUTS - n, sent_gain, 0)

    @pl.when(n > 0)
    def _():
        to_next().wait_recv()

    @pl.when(n < CUTS - 1)
    def _():
        to_next().wait_send()

    @pl.when(n == 0)
    def _():
        keep_initial().wait()


def body(old_starts, initial, blade_force, blade_owner):
    hbm = pl.BlockSpec(memory_space=pl.ANY)
    f32 = jnp.float32
    dma = pltpu.SemaphoreType.DMA
    ends, before = pl.pallas_call(
        kernel,
        out_shape=[jax.ShapeDtypeStruct((rows, NZ), f32) for rows in (ROWS, ROWS)],
        in_specs=[hbm] * 8,
        out_specs=[pl.BlockSpec(memory_space=pltpu.VMEM), hbm],
        scratch_shapes=[
            pltpu.VMEM((ROWS, NZ), f32),
            pltpu.SMEM((STEPS, CUTS), jnp.int32),
            pltpu.VMEM((NZ, 3 * NZ), jnp.bfloat16),
            pltpu.VMEM((3 * NZ, NZ), jnp.bfloat16),
            pltpu.VMEM((3 * NZ // 2, NZ), jnp.bfloat16),
            pltpu.VMEM((16, LANES), f32),
            pltpu.VMEM((3 * LANES, NZ), f32),
            pltpu.VMEM((SPACE, 2 * NVAR, 2, LANES), f32),
            pltpu.VMEM((SPACE, 2 * NVAR, 2, LANES), f32),
            pltpu.VMEM((2 * NVAR * SPACE, LANES), f32),
            pltpu.VMEM((2 * NVAR * SPACE, LANES), f32),
            pltpu.VMEM((SPACE, NVAR, 2, LANES), f32),
            pltpu.VMEM((SPACE, NVAR, 2, LANES), f32),
            pltpu.VMEM((SPACE, 2, LANES), f32),
            pltpu.VMEM((SPACE, 2, LANES), f32),
            pltpu.VMEM((SPACE, 2, 2, LANES), f32),
            pltpu.VMEM((SPACE, 2, 2, LANES), f32),
            pltpu.VMEM((8 * NVAR, LANES), f32),
            pltpu.VMEM((CUTS, 8 * NVAR, LANES), f32),
            pltpu.VMEM((ROWS, NZ), f32),
            dma((8,)),
            dma,
            dma,
            dma,
            dma,
            dma,
            dma,
            dma((CUTS,)),
            dma((CUTS,)),
            dma,
            dma,
            dma,
            dma,
            dma,
        ],
        compiler_params=pltpu.CompilerParams(
            collective_id=0, has_side_effects=True, vmem_limit_bytes=54800 * 1024
        ),
    )(
        old_starts.reshape(ROWS, NZ),
        initial.reshape(ROWS, NZ),
        blade_force.reshape(ROWS, NZ),
        blade_owner.T,
        jnp.asarray(np.ascontiguousarray(stack_table(FORWARD.T).T)),
        jnp.asarray(stack_table(FORWARD)),
        jnp.asarray(stack_table(BACK_COARSE)),
        jnp.asarray(LANE_TABLE),
    )
    shape = old_starts.shape
    return ends.reshape(shape), old_starts - before.reshape(shape)


def solution(mesh):
    placed = (
        P("cuts", None, "space", None, None),
        P(None, "space", None, None),
        P(None, "space", None, None),
        P(),
    )
    return jax.shard_map(
        body,
        mesh=mesh,
        in_specs=placed,
        out_specs=(P("cuts", None, "space", None, None), P("cuts", None, "space", None, None)),
        check_vma=False,
    )
```

```python
import functools

import jax
import jax.numpy as jnp
import numpy as np
from jax import lax
from jax.experimental import pallas as pl
from jax.experimental.pallas import tpu as pltpu
from jax.sharding import PartitionSpec as P

MESH = pl.DeviceIdType.MESH

STEPS = 3
NVAR = 5
NY = 16
NZ = 256
SPACE = 32
CUTS = 16
LANES = 128
ROWS = 2 * NVAR * NY

mach = 0.3
courant = 0.2
coarse_courant = 0.3


def wave(count, k, phase):
    angle = 2.0 * np.pi * k * np.arange(count) / count
    v = np.cos(angle) if phase == 0 else np.sin(angle)
    return v / np.sqrt(np.sum(v * v))


def group_waves(g):
    if g == 0:
        fine = [(0, 0), (64, 0), (128, 0), (64, 1)]
        coarse = [(0, 0), (64, 0)]
    else:
        fine = [(g, 0), (128 - g, 0), (g, 1), (128 - g, 1)]
        coarse = [(g, 0), (g, 1)]
    return fine, coarse


def make_tables():
    half = NZ // 2
    restrict_z = np.zeros((half, NZ))
    for j in range(half):
        restrict_z[j, 2 * j : 2 * j + 2] = 0.5
    forward = np.zeros((8, SPACE, NZ))
    back_coarse = np.zeros((4, SPACE, NZ))
    lanes = np.zeros((SPACE, 16, 8, NY))
    even = (np.arange(NY) % 2 == 0).astype(np.float64)
    for t in range(SPACE):
        for q in range(2):
            fine, coarse = group_waves(t + 32 * q)
            basis = [wave(NZ, *w) for w in fine]
            coarse_basis = [wave(half, *w) for w in coarse]
            for i in range(4):
                slot = q + 2 * i
                forward[slot, t] = basis[i]
                upper, lower = np.roll(basis[i], -1), np.roll(basis[i], 1)
                lanes[t, 0, slot] = basis[i] @ (upper + lower) - 2.0
                partner = basis[(i + 2) % 4]
                lanes[t, 1, slot] = basis[i] @ (np.roll(partner, -1) - np.roll(partner, 1))
            for i in range(2):
                slot = q + 4 * i
                back_coarse[q + 2 * i, t] = np.repeat(coarse_basis[i], 2)
                upper, lower = np.roll(coarse_basis[i], -1), np.roll(coarse_basis[i], 1)
                lanes[t, 2, slot] = coarse_basis[i] @ (upper + lower) - 2.0
                partner = coarse_basis[1 - i]
                lanes[t, 3, slot] = coarse_basis[i] @ (np.roll(partner, -1) - np.roll(partner, 1))
                for j in range(4):
                    source = (2 * i + j) % 4
                    lanes[t, 4 + j, slot] = 0.25 * (coarse_basis[i] @ (restrict_z @ basis[source])) * even
                lanes[t, 8, slot] = even
    return (
        forward.reshape(8 * SPACE, NZ).astype(np.float32),
        back_coarse.reshape(4 * SPACE, NZ).astype(np.float32),
        lanes.reshape(SPACE, 16, LANES).astype(np.float32),
    )


FORWARD, BACK_COARSE, LANE_TABLE = make_tables()
GATHER_ORDER = (12, 13, 11, 14, 10, 15, 9, 8, 7, 6, 5, 4, 3, 2, 1)


def in_two(a):
    high = a.astype(jnp.bfloat16)
    return high, (a - high.astype(jnp.float32)).astype(jnp.bfloat16)


def stack_table(a):
    high = a.astype(jnp.bfloat16)
    low = (a - high.astype(np.float32)).astype(jnp.bfloat16)
    return np.concatenate([high, high, low], axis=0)


def times_table(a, table):
    high, low = in_two(a)
    return jnp.dot(jnp.concatenate([high, low, high], axis=1), table, preferred_element_type=jnp.float32)


def turn(a, shift):
    return pltpu.roll(a, shift % LANES, 1)


def swap_blocks(arrays):
    arrays = list(arrays)
    block = lax.broadcasted_iota(jnp.int32, arrays[0].shape, 1) // NY
    for bit in (4, 2, 1):
        low = (block // bit) % 2 == 0
        for i in range(8):
            if i & bit == 0:
                a, b = arrays[i], arrays[i + bit]
                arrays[i] = jnp.where(low, a, turn(b, NY * bit))
                arrays[i + bit] = jnp.where(low, turn(a, -NY * bit), b)
    return arrays


def along_y(a, step):
    y = lax.broadcasted_iota(jnp.int32, a.shape, 1) % NY
    upper = jnp.where(y >= NY - step, turn(a, NY - step), turn(a, -step))
    lower = jnp.where(y < step, turn(a, step - NY), turn(a, step))
    return upper, lower


def below(a):
    row = lax.broadcasted_iota(jnp.int32, a.shape, 0)
    return jnp.where(row == 0, 0.0, pltpu.roll(a, 1, 0))


def above(a):
    row = lax.broadcasted_iota(jnp.int32, a.shape, 0)
    return jnp.where(row == a.shape[0] - 1, 0.0, pltpu.roll(a, a.shape[0] - 1, 0))


def rate_of(center, x_upper, x_lower, step, second_z, first_z, ratio):
    half = 0.5 * ratio
    own = second_z - 2.0 * (mach + 1.0) - 2.0
    rates = []
    ys = [along_y(center[v], step) for v in range(NVAR)]
    for v in range(NVAR):
        rates.append(x_upper[v] + (2.0 * mach + 1.0) * x_lower[v] + ys[v][0] + ys[v][1] + own * center[v])
    divergence = (x_upper[1] - x_lower[1]) + (ys[2][0] - ys[2][1]) + first_z * turn(center[3], 64)
    rates[0] = rates[0] - divergence
    rates[1] = rates[1] - (x_upper[4] - x_lower[4])
    rates[2] = rates[2] - (ys[4][0] - ys[4][1])
    rates[3] = rates[3] - first_z * turn(center[4], 64)
    rates[4] = rates[4] - divergence
    return [half * r for r in rates]


def kernel(
    old_hbm, init_hbm, force_hbm, owner_hbm, forward_hbm, inverse_hbm, back_hbm, table_hbm,
    ends, before_hbm,
    init_ref, owner_ref, forward_ref, inverse_ref, back_ref, table, stacked, out1, in1, state, first, out2, in2, out3, in3, out6, in6, packed, gathered, fine,
    load, send1, recv1, send2, recv2, send3, recv3, send4, recv4, send5, recv5, send6, recv6, store,
):
    n = lax.axis_index("cuts")
    s = lax.axis_index("space")

    def peer_of(k):
        return lax.rem(s + SPACE // 2 + (k // 2) * (1 - 2 * lax.rem(k, 2)), SPACE)

    old_ref = stacked.at[0:ROWS]
    loads = [
        pltpu.make_async_copy(source, target, load.at[i])
        for i, (source, target) in enumerate(
            (
                (forward_hbm, forward_ref),
                (old_hbm, old_ref),
                (force_hbm, stacked.at[ROWS : 2 * ROWS]),
                (init_hbm, init_ref),
                (owner_hbm, owner_ref),
                (table_hbm.at[s], table),
                (back_hbm, back_ref),
                (inverse_hbm, inverse_ref),
            )
        )
    ]
    barrier = pltpu.get_barrier_semaphore()

    def greet_space(k, c):
        pl.semaphore_signal(barrier, inc=1, device_id={"space": peer_of(k)}, device_id_type=MESH)
        return c

    def greet_cuts(k, c):
        pl.semaphore_signal(barrier, inc=1, device_id={"cuts": n - k}, device_id_type=MESH)
        return c

    lax.fori_loop(1, SPACE, greet_space, 0, unroll=True)
    lax.fori_loop(1, n + 1, greet_cuts, 0)

    for copy in loads:
        copy.start()

    for copy in loads[:4]:
        copy.wait()
    row = lax.broadcasted_iota(jnp.int32, (NY, NZ), 0)
    sums = []
    for v in range(NVAR):
        both = init_ref[2 * v * NY : (2 * v + 1) * NY] + init_ref[(2 * v + 1) * NY : (2 * v + 2) * NY]
        sums.append(both + pltpu.roll(both, NY - 1, 0))
    sums.append(jnp.zeros((NY, NZ), jnp.float32))
    for pair in range(3):
        merged = jnp.where(row % 2 == 0, sums[2 * pair], pltpu.roll(sums[2 * pair + 1], 1, 0))
        stacked[2 * ROWS + pair * NY : 2 * ROWS + (pair + 1) * NY] = merged
    stacked[2 * ROWS + 3 * NY :] = jnp.zeros((NY, NZ), jnp.float32)
    for tile in range(3):
        high, low = in_two(stacked[tile * LANES : (tile + 1) * LANES])
        modes = lax.dot_general(
            forward_ref[...],
            jnp.concatenate([high, low, high], axis=1),
            (((1,), (1,)), ((), ())),
            preferred_element_type=jnp.float32,
        )
        by_row = swap_blocks([modes[m * SPACE : (m + 1) * SPACE] for m in range(8)])
        for r in range(8):
            at = 8 * tile + r
            if at < 4 * NVAR:
                out1[:, at // 2, at % 2, :] = by_row[r]
            else:
                out6[:, at // 2 - 2 * NVAR, at % 2, :] = by_row[r]

    pl.semaphore_wait(barrier, SPACE - 1 + CUTS - 1 - n)

    def exchange(source, target, send, recv):
        def start(k, c):
            peer = peer_of(k)
            pltpu.make_async_remote_copy(
                source.at[peer], target.at[s], send, recv, device_id={"space": peer}, device_id_type=MESH
            ).start()
            return c

        def begin():
            lax.fori_loop(1, SPACE, start, 0, unroll=True)
            target[s] = source[s]

        def finish():
            others = pl.ds(0, SPACE - 1)
            pltpu.make_async_remote_copy(
                source.at[others], target.at[others], send, recv, device_id={"space": peer_of(1)}, device_id_type=MESH
            ).wait()

        return begin, finish

    begin1, finish1 = exchange(out1, in1, send1, recv1)
    begin6, finish6 = exchange(out6, in6, send6, recv6)
    begin1()
    for copy in loads[4:]:
        copy.wait()
    finish1()

    lane = [jnp.broadcast_to(table[i : i + 1], (SPACE, LANES)) for i in range(9)]

    def arrived(r):
        if r < 4 * NVAR:
            return in1[:, r // 2, r % 2, :]
        return in6[:, r // 2 - 2 * NVAR, r % 2, :]

    def restrict_modes(t):
        return lane[4] * t + lane[5] * turn(t, 96) + lane[6] * turn(t, 64) + lane[7] * turn(t, 32)

    def restrict(q0, q1):
        t = q0 + q1
        return restrict_modes(t + turn(t, -1))

    def fine_rate(ref):
        q = [[ref[(2 * v + i) * SPACE : (2 * v + i + 1) * SPACE] for i in range(2)] for v in range(NVAR)]
        low = rate_of(
            [q[v][0] for v in range(NVAR)], [q[v][1] for v in range(NVAR)], [below(q[v][1]) for v in range(NVAR)],
            1, lane[0], lane[1], courant,
        )
        high = rate_of(
            [q[v][1] for v in range(NVAR)], [above(q[v][0]) for v in range(NVAR)], [q[v][0] for v in range(NVAR)],
            1, lane[0], lane[1], courant,
        )
        return q, [[low[v], high[v]] for v in range(NVAR)]

    def coarse_advance(c):
        r = rate_of(c, [above(a) for a in c], [below(a) for a in c], 2, lane[2], lane[3], coarse_courant)
        return [c[v] + r[v] for v in range(NVAR)]

    for r in range(2 * NVAR):
        state[r * SPACE : (r + 1) * SPACE] = arrived(r)
    place = lax.broadcasted_iota(jnp.int32, (SPACE, LANES), 0)
    hits = [(place == owner_ref[k, n]).astype(jnp.float32) for k in range(STEPS)]
    old_coarse = [restrict(arrived(2 * v), arrived(2 * v + 1)) for v in range(NVAR)]
    for k in range(STEPS):
        q, rates = fine_rate(state)
        scale = courant * hits[k]
        for v in range(NVAR):
            for i in range(2):
                at = slice((2 * v + i) * SPACE, (2 * v + i + 1) * SPACE)
                source = scale * arrived(2 * NVAR + 2 * v + i)
                first[at] = q[v][i] + rates[v][i] + source
        q1, rates1 = fine_rate(first)
        for v in range(NVAR):
            for i in range(2):
                at = slice((2 * v + i) * SPACE, (2 * v + i + 1) * SPACE)
                source = scale * arrived(2 * NVAR + 2 * v + i)
                state[at] = 0.5 * (state[at] + q1[v][i] + rates1[v][i] + source)

    final = [[state[(2 * v + i) * SPACE : (2 * v + i + 1) * SPACE] for i in range(2)] for v in range(NVAR)]
    count = hits[0] + hits[1] + hits[2]
    coarse_source = [
        courant * count * restrict(arrived(2 * NVAR + 2 * v), arrived(2 * NVAR + 2 * v + 1)) for v in range(NVAR)
    ]
    guess_old = [a + b for a, b in zip(coarse_advance(old_coarse), coarse_source)]
    for v in range(NVAR):
        gain = coarse_source[v] + restrict(final[v][0], final[v][1]) - guess_old[v]
        packed[8 * v : 8 * v + 8] = (
            gain[0:8] + turn(gain[8:16], 1) + turn(gain[16:24], 32) + turn(gain[24:32], 33)
        )

    def send_gain(k):
        return pltpu.make_async_remote_copy(
            packed, gathered.at[n], send4.at[k], recv4.at[n], device_id={"cuts": n + k}, device_id_type=MESH
        )

    for k in GATHER_ORDER:
        @pl.when(n + k < CUTS)
        def _():
            send_gain(k).start()

    begin6()

    for v in range(NVAR):
        for i in range(2):
            out2[:, v, i, :] = final[v][i]
    begin2, finish2 = exchange(out2, in2, send2, recv2)
    begin2()

    useful = lane[8][0:8]

    def advance(m, c):
        pltpu.make_async_remote_copy(
            packed, gathered.at[m], send4.at[0], recv4.at[m], device_id={"cuts": m}, device_id_type=MESH
        ).wait_recv()
        moved = coarse_advance(list(c))
        result = []
        for v in range(NVAR):
            g = gathered[m, 8 * v : 8 * v + 8]
            parts = [useful * g, useful * turn(g, -1), useful * turn(g, -32), useful * turn(g, -33)]
            result.append(moved[v] + jnp.concatenate(parts, axis=0))
        return tuple(result)

    finish6()
    begin_coarse = []
    for v in range(NVAR):
        a = arrived(4 * NVAR + v // 2)
        begin_coarse.append(restrict_modes(turn(a, -1) if v % 2 else a))
    start = lax.fori_loop(0, n, advance, tuple(begin_coarse))
    guess_new = [a + b for a, b in zip(coarse_advance(list(start)), coarse_source)]
    change = [guess_new[v] - guess_old[v] for v in range(NVAR)]
    out3[:, 0, :] = change[0] + turn(change[1], 1) + turn(change[2], 32) + turn(change[3], 33)
    out3[:, 1, :] = change[4]
    begin3, finish3 = exchange(out3, in3, send3, recv3)
    begin3()

    finish2()
    halves = []
    for tile in range(2):
        rows = []
        for r in range(8):
            from_row = min(8 * tile + r, 2 * NVAR - 1)
            rows.append(in2[:, from_row // 2, from_row % 2, :])
        halves.append(jnp.concatenate(swap_blocks(rows), axis=0).T)
    modes = jnp.concatenate([halves[0], halves[1][: ROWS - LANES]], axis=0)
    fine[...] = times_table(modes, inverse_ref[...])

    def to_next():
        return pltpu.make_async_remote_copy(
            fine, before_hbm, send5, recv5, device_id={"cuts": lax.rem(n + 1, CUTS)}, device_id_type=MESH
        )

    def keep_initial():
        return pltpu.make_async_copy(init_ref, before_hbm, store)

    @pl.when(n < CUTS - 1)
    def _():
        to_next().start()

    @pl.when(n == 0)
    def _():
        keep_initial().start()

    finish3()
    mask = jnp.broadcast_to(useful[0:1], (SPACE, LANES))
    four = in3[:, 0, :]
    rows = [mask * a for a in (four, turn(four, -1), turn(four, -32), turn(four, -33))] + [in3[:, 1, :]]
    rows = [a + turn(a, 1) for a in rows]
    by_mode = swap_blocks(rows + rows[4:] * 3)
    change = jnp.concatenate([by_mode[0], by_mode[1], by_mode[4], by_mode[5]], axis=0).T
    change = times_table(change[: NVAR * NY], back_ref[...])
    for v in range(NVAR):
        for i in range(2):
            at = slice((2 * v + i) * NY, (2 * v + i + 1) * NY)
            ends[at] = fine[at] + change[v * NY : (v + 1) * NY]
    def sent_gain(k, c):
        send_gain(k).wait_send()
        return c

    lax.fori_loop(1, CUTS - n, sent_gain, 0)

    @pl.when(n > 0)
    def _():
        to_next().wait_recv()

    @pl.when(n < CUTS - 1)
    def _():
        to_next().wait_send()

    @pl.when(n == 0)
    def _():
        keep_initial().wait()


def body(old_starts, initial, blade_force, blade_owner):
    hbm = pl.BlockSpec(memory_space=pl.ANY)
    f32 = jnp.float32
    dma = pltpu.SemaphoreType.DMA
    ends, before = pl.pallas_call(
        kernel,
        out_shape=[jax.ShapeDtypeStruct((rows, NZ), f32) for rows in (ROWS, ROWS)],
        in_specs=[hbm] * 8,
        out_specs=[pl.BlockSpec(memory_space=pltpu.VMEM), hbm],
        scratch_shapes=[
            pltpu.VMEM((ROWS, NZ), f32),
            pltpu.SMEM((STEPS, CUTS), jnp.int32),
            pltpu.VMEM((NZ, 3 * NZ), jnp.bfloat16),
            pltpu.VMEM((3 * NZ, NZ), jnp.bfloat16),
            pltpu.VMEM((3 * NZ // 2, NZ), jnp.bfloat16),
            pltpu.VMEM((16, LANES), f32),
            pltpu.VMEM((3 * LANES, NZ), f32),
            pltpu.VMEM((SPACE, 2 * NVAR, 2, LANES), f32),
            pltpu.VMEM((SPACE, 2 * NVAR, 2, LANES), f32),
            pltpu.VMEM((2 * NVAR * SPACE, LANES), f32),
            pltpu.VMEM((2 * NVAR * SPACE, LANES), f32),
            pltpu.VMEM((SPACE, NVAR, 2, LANES), f32),
            pltpu.VMEM((SPACE, NVAR, 2, LANES), f32),
            pltpu.VMEM((SPACE, 2, LANES), f32),
            pltpu.VMEM((SPACE, 2, LANES), f32),
            pltpu.VMEM((SPACE, 2, 2, LANES), f32),
            pltpu.VMEM((SPACE, 2, 2, LANES), f32),
            pltpu.VMEM((8 * NVAR, LANES), f32),
            pltpu.VMEM((CUTS, 8 * NVAR, LANES), f32),
            pltpu.VMEM((ROWS, NZ), f32),
            dma((8,)),
            dma,
            dma,
            dma,
            dma,
            dma,
            dma,
            dma((CUTS,)),
            dma((CUTS,)),
            dma,
            dma,
            dma,
            dma,
            dma,
        ],
        compiler_params=pltpu.CompilerParams(
            collective_id=0, has_side_effects=True, vmem_limit_bytes=54800 * 1024
        ),
    )(
        old_starts.reshape(ROWS, NZ),
        initial.reshape(ROWS, NZ),
        blade_force.reshape(ROWS, NZ),
        blade_owner.T,
        jnp.asarray(np.ascontiguousarray(stack_table(FORWARD.T).T)),
        jnp.asarray(stack_table(FORWARD)),
        jnp.asarray(stack_table(BACK_COARSE)),
        jnp.asarray(LANE_TABLE),
    )
    shape = old_starts.shape
    return ends.reshape(shape), old_starts - before.reshape(shape)


def solution(mesh):
    placed = (
        P("cuts", None, "space", None, None),
        P(None, "space", None, None),
        P(None, "space", None, None),
        P(),
    )
    return jax.shard_map(
        body,
        mesh=mesh,
        in_specs=placed,
        out_specs=(P("cuts", None, "space", None, None), P("cuts", None, "space", None, None)),
        check_vma=False,
    )
```
